32 devices in a mesh: inp: 16 (over z, x, core), chan: 2 (over y).
Axes of the slice: x: 2, y: 2, z: 4, core: 2. Of those that a mesh axis runs over, the one named last changes fastest.
Arguments:
- voltages: bfloat16 [2, 4, 1024, 2048], P(None, None, ('inp', 'chan')), may hold values from -32 to 32
- positions: float32 [1024, 2], replicated, may hold values from -8 to 8
- directions: float32 [1024, 2], replicated, may hold values from -0.5 to 0.5
- basis: float32 [2, 4, 16, 1024], P(None, 'chan', None, 'inp'), may hold values from -6 to 6
- rank_count: int32 [4], P('chan'), may hold values from 1 to 16, as said below
Outputs:
- beam_power: float32 [1024, 4, 128], P('inp', 'chan')
The draws below stay inside these ranges and needn't reach their ends.
Inputs may be any that keep to these rules, and one draw needn't show every extreme that they name: `rank_count`: each channel uses at least one basis vector, and some channel uses all 16.
All inputs are finite; a program needn't handle non-finite values.
Results may differ from the reference program's by a relative error of at most 0.0023.
Values may be sent and summed in bfloat16 or wider, within the bound.
A program may use at most 64 MiB of HBM per device.

```python
import math
import jax
import jax.numpy as jnp
from jax import lax

INPUTS = 1024
BEAMS = 1024
RANK = 16
DS = 16
CHANNELS = 4
FRAMES = 2048
TIMES = 128


def interference_basis(key):
    values = jax.random.normal(jax.random.fold_in(key, 7), (2, CHANNELS, RANK, INPUTS), jnp.float32)
    return jnp.clip(values, -6.0, 6.0)


def draw_basis(key, part):
    return interference_basis(key)


def draw_voltages(key, part):
    full_shape = (2, CHANNELS, INPUTS, FRAMES)
    noise_part = jnp.clip(jax.random.normal(jax.random.fold_in(key, 11), full_shape, jnp.float32), -6.0, 6.0)
    basis_rows = interference_basis(key)
    signal = jax.random.normal(jax.random.fold_in(key, 13), (2, CHANNELS, RANK, FRAMES), jnp.float32) * 0.35
    total_real = noise_part[0]
    total_imag = noise_part[1]
    for column in range(RANK):
        basis_real = basis_rows[0, :, column, :][:, :, None]
        basis_imag = basis_rows[1, :, column, :][:, :, None]
        signal_real = signal[0, :, column, :][:, None, :]
        signal_imag = signal[1, :, column, :][:, None, :]
        total_real = total_real + (basis_real * signal_real - basis_imag * signal_imag)
        total_imag = total_imag + (basis_real * signal_imag + basis_imag * signal_real)
    return jnp.clip(jnp.stack([total_real, total_imag]), -32.0, 32.0).astype(jnp.bfloat16)


def draw_rank_count(key, part):
    counts = jax.random.randint(jax.random.fold_in(key, 21), (CHANNELS,), 1, RANK + 1)
    chosen = jax.random.randint(jax.random.fold_in(key, 22), (), 0, CHANNELS)
    return jnp.where(jnp.arange(CHANNELS) == chosen, RANK, counts).astype(jnp.int32)


def setup_inputs(seed: int = 0) -> dict:
    arg_keys = jax.random.split(jax.random.key(seed), 6)
    return {
        "voltages": draw_voltages(jax.random.fold_in(arg_keys[5], 71), 0),
        "positions": jnp.clip(jax.random.uniform(arg_keys[1], (INPUTS, 2), jnp.float32, -8.0, 8.0), -8.0, 8.0),
        "directions": jnp.clip(jax.random.uniform(arg_keys[2], (BEAMS, 2), jnp.float32, -0.5, 0.5), -0.5, 0.5),
        "basis": draw_basis(jax.random.fold_in(arg_keys[5], 71), 0),
        "rank_count": draw_rank_count(jax.random.fold_in(arg_keys[5], 71), 0),
    }


HIGHEST_PRECISION = lax.Precision.HIGHEST

def orthonormal(basis_rows, rank_used):
    ranks = basis_rows.shape[1]
    active = (jnp.arange(ranks) < rank_used).astype(basis_rows.dtype)

    def build_column(column_index, ortho_rows):
        real_part = lax.dynamic_index_in_dim(basis_rows[0], column_index, 0, keepdims=False)
        imag_part = lax.dynamic_index_in_dim(basis_rows[1], column_index, 0, keepdims=False)
        for second in range(2):
            coef_real = jnp.dot(ortho_rows[0], real_part, precision=HIGHEST_PRECISION) + jnp.dot(ortho_rows[1], imag_part, precision=HIGHEST_PRECISION)
            coef_imag = jnp.dot(ortho_rows[0], imag_part, precision=HIGHEST_PRECISION) - jnp.dot(ortho_rows[1], real_part, precision=HIGHEST_PRECISION)
            real_part = real_part - (jnp.dot(coef_real, ortho_rows[0], precision=HIGHEST_PRECISION) - jnp.dot(coef_imag, ortho_rows[1], precision=HIGHEST_PRECISION))
            imag_part = imag_part - (jnp.dot(coef_real, ortho_rows[1], precision=HIGHEST_PRECISION) + jnp.dot(coef_imag, ortho_rows[0], precision=HIGHEST_PRECISION))
        flag = lax.dynamic_index_in_dim(active, column_index, 0, keepdims=False)
        normalize = flag / jnp.sqrt(jnp.sum(real_part * real_part + imag_part * imag_part) + (1.0 - flag))
        new_column = jnp.stack([real_part * normalize, imag_part * normalize])[:, None, :]
        return lax.dynamic_update_slice_in_dim(ortho_rows, new_column, column_index, 1)
    return lax.fori_loop(0, ranks, build_column, jnp.zeros_like(basis_rows))

def half_dot(left, right):
    return jnp.dot(left, right, preferred_element_type=jnp.float32)

def steer_block(row_start, row_count, positions, directions, ortho_rows, frequency):
    chosen = lax.dynamic_slice_in_dim(directions, row_start, row_count, 0)
    phase_angle = 2.0 * jnp.pi * frequency * (chosen[:, 0:1] * positions[:, 0][None, :] + chosen[:, 1:2] * positions[:, 1][None, :])
    inverse = 1.0 / math.sqrt(positions.shape[0])
    steer_real = jnp.cos(phase_angle) * inverse
    steer_imag = -jnp.sin(phase_angle) * inverse
    short_real = steer_real.astype(jnp.bfloat16)
    short_imag = steer_imag.astype(jnp.bfloat16)
    ortho_real = ortho_rows[0].astype(jnp.bfloat16)
    ortho_imag = ortho_rows[1].astype(jnp.bfloat16)
    along_real = (half_dot(short_real, ortho_real.T) - half_dot(short_imag, ortho_imag.T)).astype(jnp.bfloat16)
    along_imag = (half_dot(short_real, ortho_imag.T) + half_dot(short_imag, ortho_real.T)).astype(jnp.bfloat16)
    kept_real = steer_real - (half_dot(along_real, ortho_real) + half_dot(along_imag, ortho_imag))
    kept_imag = steer_imag - (half_dot(along_imag, ortho_real) - half_dot(along_real, ortho_imag))
    return (kept_real.astype(jnp.bfloat16), kept_imag.astype(jnp.bfloat16))

def detect(weight_real, weight_imag, volt_real, volt_imag):
    stacked = jnp.concatenate([volt_real, volt_imag], axis=1)
    frame_count = volt_real.shape[1]
    from_real = jnp.dot(weight_real, stacked, preferred_element_type=jnp.float32)
    from_imag = jnp.dot(weight_imag, stacked, preferred_element_type=jnp.float32)
    beam_real = from_real[:, :frame_count] - from_imag[:, frame_count:]
    beam_imag = from_real[:, frame_count:] + from_imag[:, :frame_count]
    return beam_real * beam_real + beam_imag * beam_imag

def reference(voltages, positions, directions, basis, rank_count):
    channels = voltages.shape[1]

    def one_channel(channel):
        channel_volts = lax.dynamic_index_in_dim(voltages, channel, 1, keepdims=False)
        channel_basis = lax.dynamic_index_in_dim(basis, channel, 1, keepdims=False)
        rank_used = lax.dynamic_index_in_dim(rank_count, channel, 0, keepdims=False)
        ortho_rows = orthonormal(channel_basis, rank_used)
        frequency = 1.0 + 0.5 * channel.astype(jnp.float32) / channels
        weight_real, weight_imag = steer_block(0, BEAMS, positions, directions, ortho_rows, frequency)
        detected = detect(weight_real, weight_imag, channel_volts[0], channel_volts[1])
        return lax.optimization_barrier(jnp.mean(detected.reshape(BEAMS, TIMES, DS), axis=2))
    result = lax.map(one_channel, jnp.arange(channels, dtype=jnp.int32))
    return jnp.transpose(result, (1, 0, 2))
```

```python
import functools
import math

import jax
import jax.numpy as jnp
import numpy as np
from jax import lax
from jax.experimental import pallas as pl
from jax.experimental.pallas import tpu as pltpu
from jax.sharding import PartitionSpec as P

FGROUPS = 8
DS = 16
ROWS = 128
MESH = pl.DeviceIdType.MESH


HIGHEST_PRECISION = lax.Precision.HIGHEST


def orthonormal(basis_rows, rank_used):
    ranks = basis_rows.shape[1]
    active = (jnp.arange(ranks) < rank_used).astype(basis_rows.dtype)

    def build_column(column_index, ortho_rows):
        real_part = lax.dynamic_index_in_dim(basis_rows[0], column_index, 0, keepdims=False)
        imag_part = lax.dynamic_index_in_dim(basis_rows[1], column_index, 0, keepdims=False)
        for second in range(2):
            coef_real = jnp.dot(ortho_rows[0], real_part, precision=HIGHEST_PRECISION) + jnp.dot(
                ortho_rows[1], imag_part, precision=HIGHEST_PRECISION
            )
            coef_imag = jnp.dot(ortho_rows[0], imag_part, precision=HIGHEST_PRECISION) - jnp.dot(
                ortho_rows[1], real_part, precision=HIGHEST_PRECISION
            )
            real_part = real_part - (
                jnp.dot(coef_real, ortho_rows[0], precision=HIGHEST_PRECISION)
                - jnp.dot(coef_imag, ortho_rows[1], precision=HIGHEST_PRECISION)
            )
            imag_part = imag_part - (
                jnp.dot(coef_real, ortho_rows[1], precision=HIGHEST_PRECISION)
                + jnp.dot(coef_imag, ortho_rows[0], precision=HIGHEST_PRECISION)
            )
        flag = lax.dynamic_index_in_dim(active, column_index, 0, keepdims=False)
        normalize = flag / jnp.sqrt(
            jnp.sum(real_part * real_part + imag_part * imag_part) + (1.0 - flag)
        )
        new_column = jnp.stack([real_part * normalize, imag_part * normalize])[:, None, :]
        return lax.dynamic_update_slice_in_dim(ortho_rows, new_column, column_index, 1)

    return lax.fori_loop(0, ranks, build_column, jnp.zeros_like(basis_rows))


def half_dot(left, right):
    return jnp.dot(left, right, preferred_element_type=jnp.float32)


def steer_block(row_start, row_count, positions, directions, ortho_rows, frequency):
    chosen = lax.dynamic_slice_in_dim(directions, row_start, row_count, 0)
    phase_angle = (
        2.0
        * jnp.pi
        * frequency
        * (chosen[:, 0:1] * positions[:, 0][None, :] + chosen[:, 1:2] * positions[:, 1][None, :])
    )
    inverse = 1.0 / math.sqrt(positions.shape[0])
    steer_real = jnp.cos(phase_angle) * inverse
    steer_imag = -jnp.sin(phase_angle) * inverse
    short_real = steer_real.astype(jnp.bfloat16)
    short_imag = steer_imag.astype(jnp.bfloat16)
    ortho_real = ortho_rows[0].astype(jnp.bfloat16)
    ortho_imag = ortho_rows[1].astype(jnp.bfloat16)
    along_real = (half_dot(short_real, ortho_real.T) - half_dot(short_imag, ortho_imag.T)).astype(
        jnp.bfloat16
    )
    along_imag = (half_dot(short_real, ortho_imag.T) + half_dot(short_imag, ortho_real.T)).astype(
        jnp.bfloat16
    )
    kept_real = steer_real - (half_dot(along_real, ortho_real) + half_dot(along_imag, ortho_imag))
    kept_imag = steer_imag - (half_dot(along_imag, ortho_real) - half_dot(along_real, ortho_imag))
    return (kept_real.astype(jnp.bfloat16), kept_imag.astype(jnp.bfloat16))


def projected_weights(positions, directions, ortho_rows, frequency):
    beam_count = directions.shape[0]
    row_count = min(beam_count, 512)
    block_count = beam_count // row_count

    def one_block(block_index):
        return steer_block(
            block_index * row_count, row_count, positions, directions, ortho_rows, frequency
        )

    weight_real, weight_imag = lax.map(one_block, jnp.arange(block_count, dtype=jnp.int32))
    input_count = positions.shape[0]
    return (
        weight_real.reshape(beam_count, input_count),
        weight_imag.reshape(beam_count, input_count),
    )


def detect(weight_real, weight_imag, volt_real, volt_imag):
    stacked = jnp.concatenate([volt_real, volt_imag], axis=1)
    frame_count = volt_real.shape[1]
    from_real = jnp.dot(weight_real, stacked, preferred_element_type=jnp.float32)
    from_imag = jnp.dot(weight_imag, stacked, preferred_element_type=jnp.float32)
    beam_real = from_real[:, :frame_count] - from_imag[:, frame_count:]
    beam_imag = from_real[:, frame_count:] + from_imag[:, :frame_count]
    return beam_real * beam_real + beam_imag * beam_imag


def shards(voltages, positions, directions, basis, rank_count):
    inp_size = lax.axis_size("inp")
    chan_size = lax.axis_size("chan")
    per_chan = inp_size // FGROUPS
    channels = chan_size * per_chan
    local_inputs = voltages.shape[2]
    frames_dev = voltages.shape[3] // FGROUPS
    input_count = positions.shape[0]
    beam_count = directions.shape[0]
    sub_channel = lax.axis_index("inp") // FGROUPS
    channel = lax.axis_index("chan") * per_chan + sub_channel
    frequency = 1.0 + 0.5 * channel.astype(jnp.float32) / channels
    rank_used = jnp.sum(jnp.where(jnp.arange(per_chan) == sub_channel, rank_count, 0))
    group_basis = lax.all_gather(basis, "inp", axis=3, tiled=True)
    own_basis = lax.dynamic_index_in_dim(group_basis, sub_channel, 1, keepdims=False)
    sectioned = voltages.reshape(2, chan_size, per_chan, local_inputs, FGROUPS, frames_dev)
    sectioned = jnp.transpose(sectioned, (0, 1, 2, 4, 3, 5)).reshape(
        2, chan_size, inp_size, local_inputs, frames_dev
    )
    ordered_positions = jnp.transpose(
        positions.reshape(inp_size, chan_size, local_inputs, 2), (1, 0, 2, 3)
    ).reshape(input_count, 2)
    ordered_basis = own_basis.reshape(2, own_basis.shape[1], inp_size, chan_size, local_inputs)
    ordered_basis = jnp.transpose(ordered_basis, (0, 1, 3, 2, 4)).reshape(
        2, own_basis.shape[1], input_count
    )
    ortho_rows = orthonormal(ordered_basis, rank_used)
    weight_real, weight_imag = projected_weights(
        ordered_positions, directions, ortho_rows, frequency
    )
    turned = lax.all_to_all(
        lax.all_to_all(sectioned, "inp", split_axis=2, concat_axis=3, tiled=True),
        "chan",
        split_axis=1,
        concat_axis=3,
        tiled=True,
    )
    detected = detect(weight_real, weight_imag, turned[0, 0, 0], turned[1, 0, 0])
    binned = jnp.mean(detected.reshape(beam_count, frames_dev // DS, DS), axis=2)
    regrouped = lax.all_to_all(binned[:, None, :], "inp", split_axis=0, concat_axis=1, tiled=True)
    return regrouped.reshape(beam_count // inp_size, per_chan, FGROUPS * (frames_dev // DS))


def turn_coefficients(input_count):
    nodes = np.cos(np.pi * (np.arange(400) + 0.5) / 400) * 0.25 * 0.5 + 0.125
    root = np.sqrt(nodes)
    scale = 1.0 / math.sqrt(input_count)
    fit = np.polynomial.chebyshev.Chebyshev.fit
    power = np.polynomial.Polynomial
    sin_fit = fit(nodes, np.sin(2 * np.pi * root) / root, 6, domain=[0, 0.25]).convert(kind=power)
    cos_fit = fit(nodes, np.cos(2 * np.pi * root), 7, domain=[0, 0.25]).convert(kind=power)
    return (
        [float(value) * scale for value in sin_fit.coef],
        [float(value) * scale for value in cos_fit.coef],
    )


def horner(coefs, x):
    total = jnp.full_like(x, coefs[-1])
    for value in coefs[-2::-1]:
        total = total * x + value
    return total


def across(left, right):
    return lax.dot_general(
        left, right, (((1,), (1,)), ((), ())), preferred_element_type=jnp.float32
    )


def fused_kernel(
    sizes,
    volt_ref,
    pos_ref,
    dir_ref,
    basis_ref,
    rank_ref,
    out_ref,
    turned,
    basis_in,
    rows_real,
    rows_imag,
    ortho_real,
    ortho_imag,
    ortho_half,
    weight_real,
    weight_imag,
    power_out,
    power_in,
    local_sem,
    volt_send,
    volt_recv,
    basis_send,
    basis_recv,
    power_send,
    power_recv,
):
    inp_size, chan_size, per_chan, beam_count, frames_dev = sizes
    devices = inp_size * chan_size
    local_inputs = volt_ref.shape[2]
    input_count = pos_ref.shape[1]
    ranks = basis_ref.shape[2]
    my_inp = lax.axis_index("inp")
    my_chan = lax.axis_index("chan")
    me = my_inp * chan_size + my_chan
    sub = my_inp // FGROUPS
    samples = frames_dev // DS
    beams_each = beam_count // inp_size
    owners = ROWS // beams_each
    blocks = beam_count // ROWS

    def device(number):
        return (number // chan_size, lax.rem(number, chan_size))

    def other(k):
        return lax.rem(me + k, devices)

    def other_inp(k):
        return lax.rem(my_inp + k, inp_size)

    barrier = pltpu.get_barrier_semaphore()

    def greet(k, carry):
        pl.semaphore_signal(barrier, inc=1, device_id=device(other(k)), device_id_type=MESH)
        return carry

    lax.fori_loop(1, devices, greet, 0)
    pl.semaphore_wait(barrier, devices - 1)

    def basis_copy(target, slot):
        return pltpu.make_async_remote_copy(
            src_ref=basis_ref.at[:, target // FGROUPS],
            dst_ref=basis_in.at[slot],
            send_sem=basis_send.at[target],
            recv_sem=basis_recv.at[slot],
            device_id=(target, my_chan),
            device_id_type=MESH,
        )

    def volt_block(target):
        target_inp = target // chan_size
        channel = lax.rem(target, chan_size) * per_chan + target_inp // FGROUPS
        start = pl.multiple_of(lax.rem(target_inp, FGROUPS) * frames_dev, frames_dev)
        return volt_ref.at[:, channel, :, pl.ds(start, frames_dev)]

    def turned_block(slot):
        return turned.at[
            :, pl.ds(pl.multiple_of(slot * local_inputs, local_inputs), local_inputs), :
        ]

    def volt_copy(target, slot):
        return pltpu.make_async_remote_copy(
            src_ref=volt_block(target),
            dst_ref=turned_block(slot),
            send_sem=volt_send.at[target],
            recv_sem=volt_recv.at[slot],
            device_id=device(target),
            device_id_type=MESH,
        )

    def power_copy(target, slot):
        return pltpu.make_async_remote_copy(
            src_ref=power_out.at[target],
            dst_ref=power_in.at[slot],
            send_sem=power_send.at[target],
            recv_sem=power_recv.at[slot],
            device_id=(target, my_chan),
            device_id_type=MESH,
        )

    def send_basis(k, carry):
        basis_copy(other_inp(k), my_inp).start()
        return carry

    lax.fori_loop(1, inp_size, send_basis, 0)

    def send_volt(k, carry):
        volt_copy(other(k), me).start()
        return carry

    lax.fori_loop(1, devices, send_volt, 0)
    own = pltpu.make_async_copy(volt_block(me), turned_block(me), local_sem)
    own.start()

    basis_in[my_inp] = basis_ref[:, sub]

    def take_basis(k, carry):
        basis_copy(other_inp(k), other_inp(k)).wait_recv()
        return carry

    lax.fori_loop(1, inp_size, take_basis, 0)
    rows_real[...] = jnp.concatenate([basis_in[s, 0] for s in range(inp_size)], axis=1)
    rows_imag[...] = jnp.concatenate([basis_in[s, 1] for s in range(inp_size)], axis=1)
    ortho_real[...] = jnp.zeros_like(ortho_real)
    ortho_imag[...] = jnp.zeros_like(ortho_imag)
    rank_used = rank_ref[sub]

    def build_row(row, carry):
        real_part = rows_real[pl.ds(row, 1), :]
        imag_part = rows_imag[pl.ds(row, 1), :]
        for second in range(2):
            real_rows, imag_rows = ortho_real[...], ortho_imag[...]
            coef_real = jnp.sum(
                real_rows * real_part + imag_rows * imag_part, axis=1, keepdims=True
            )
            coef_imag = jnp.sum(
                real_rows * imag_part - imag_rows * real_part, axis=1, keepdims=True
            )
            real_part = real_part - jnp.sum(
                coef_real * real_rows - coef_imag * imag_rows, axis=0, keepdims=True
            )
            imag_part = imag_part - jnp.sum(
                coef_real * imag_rows + coef_imag * real_rows, axis=0, keepdims=True
            )
        flag = jnp.where(row < rank_used, 1.0, 0.0).astype(jnp.float32)
        square = jnp.sum(
            real_part * real_part + imag_part * imag_part, axis=1, keepdims=True
        )
        normalize = flag / jnp.sqrt(square + (1.0 - flag))
        ortho_real[pl.ds(row, 1), :] = real_part * normalize
        ortho_imag[pl.ds(row, 1), :] = imag_part * normalize
        return carry

    lax.fori_loop(0, ranks, build_row, 0)
    ortho_half[...] = jnp.concatenate([ortho_real[...], ortho_imag[...]], axis=0).astype(
        jnp.bfloat16
    )

    channel = my_chan * per_chan + sub
    frequency = 1.0 + 0.5 * channel.astype(jnp.float32) / (chan_size * per_chan)
    sin_coefs, cos_coefs = turn_coefficients(input_count)

    def weigh(block, carry):
        rows = pl.ds(pl.multiple_of(block * ROWS, ROWS), ROWS)
        first = jnp.broadcast_to(dir_ref[0:1, rows], (ROWS, ROWS)).T
        second = jnp.broadcast_to(dir_ref[1:2, rows], (ROWS, ROWS)).T
        reals, imags = [], []
        for piece in range(input_count // ROWS):
            lanes = slice(piece * ROWS, (piece + 1) * ROWS)
            turns = first * (pos_ref[0:1, lanes] * frequency) + second * (
                pos_ref[1:2, lanes] * frequency
            )
            turns = turns - jnp.round(turns)
            square = turns * turns
            reals.append(horner(cos_coefs, square))
            imags.append(-turns * horner(sin_coefs, square))
        steer_real = jnp.concatenate(reals, axis=1)
        steer_imag = jnp.concatenate(imags, axis=1)
        half = ortho_half[...]
        from_real = across(steer_real.astype(jnp.bfloat16), half)
        from_imag = across(steer_imag.astype(jnp.bfloat16), half)
        along_real = from_real[:, :ranks] - from_imag[:, ranks:]
        along_imag = from_real[:, ranks:] + from_imag[:, :ranks]
        for_real = jnp.concatenate([along_real, along_imag], axis=1).astype(jnp.bfloat16)
        for_imag = jnp.concatenate([along_imag, -along_real], axis=1).astype(jnp.bfloat16)
        weight_real[rows, :] = (steer_real - half_dot(for_real, half)).astype(jnp.bfloat16)
        weight_imag[rows, :] = (steer_imag - half_dot(for_imag, half)).astype(jnp.bfloat16)
        return carry

    lax.fori_loop(0, blocks, weigh, 0)

    def take_volt(k, carry):
        volt_copy(other(k), other(k)).wait_recv()
        return carry

    own.wait()
    lax.fori_loop(1, devices, take_volt, 0)

    sample_row = lax.broadcasted_iota(jnp.int32, (samples, frames_dev), 0)
    frame_column = lax.broadcasted_iota(jnp.int32, (samples, frames_dev), 1)
    inside = (frame_column >= sample_row * DS) & (frame_column < sample_row * DS + DS)
    pool = jnp.where(inside, 1.0 / DS, 0.0).astype(jnp.bfloat16)

    def form(step, carry):
        block = lax.rem(step + my_inp // owners, blocks)
        rows = pl.ds(pl.multiple_of(block * ROWS, ROWS), ROWS)
        volt_real, volt_imag = turned[0], turned[1]
        left, right = weight_real[rows, :], weight_imag[rows, :]
        beam_real = half_dot(left, volt_real) - half_dot(right, volt_imag)
        beam_imag = half_dot(left, volt_imag) + half_dot(right, volt_real)
        power = beam_real * beam_real + beam_imag * beam_imag
        high = power.astype(jnp.bfloat16)
        rest = power - high.astype(jnp.float32)
        middle = rest.astype(jnp.bfloat16)
        low = (rest - middle.astype(jnp.float32)).astype(jnp.bfloat16)
        binned = across(pool, high) + across(pool, middle) + across(pool, low)
        for part in range(owners):
            target = block * owners + part
            piece = binned[:, part * beams_each : (part + 1) * beams_each]

            @pl.when(target == my_inp)
            def keep():
                power_in[my_inp] = piece

            @pl.when(target != my_inp)
            def pass_on():
                power_out[target] = piece
                power_copy(target, my_inp).start()

        return carry

    lax.fori_loop(0, blocks, form, 0)

    def take_power(k, carry):
        power_copy(other_inp(k), other_inp(k)).wait_recv()
        return carry

    lax.fori_loop(1, inp_size, take_power, 0)
    for index in range(per_chan):
        group = [power_in[index * FGROUPS + f] for f in range(FGROUPS)]
        out_ref[index] = jnp.concatenate(group, axis=0).T

    def finish_inp(k, carry):
        basis_copy(other_inp(k), my_inp).wait_send()
        power_copy(other_inp(k), my_inp).wait_send()
        return carry

    lax.fori_loop(1, inp_size, finish_inp, 0)

    def finish_volt(k, carry):
        volt_copy(other(k), me).wait_send()
        return carry

    lax.fori_loop(1, devices, finish_volt, 0)


def fused(voltages, positions, directions, basis, rank_count):
    inp_size = lax.axis_size("inp")
    chan_size = lax.axis_size("chan")
    devices = inp_size * chan_size
    per_chan = inp_size // FGROUPS
    frames_dev = voltages.shape[3] // FGROUPS
    input_count = positions.shape[0]
    beam_count = directions.shape[0]
    ranks = basis.shape[2]
    basis_lanes = basis.shape[3]
    samples = frames_dev // DS
    beams_each = beam_count // inp_size
    sizes = (inp_size, chan_size, per_chan, beam_count, frames_dev)
    vmem = pl.BlockSpec(memory_space=pltpu.VMEM)
    dma = pltpu.SemaphoreType.DMA
    row_block = pltpu.VMEM((ranks, input_count), jnp.float32)
    weight = pltpu.VMEM((beam_count, input_count), jnp.bfloat16)
    result = pl.pallas_call(
        functools.partial(fused_kernel, sizes),
        out_shape=jax.ShapeDtypeStruct(
            (per_chan, beams_each, FGROUPS * samples), jnp.float32
        ),
        in_specs=[
            pl.BlockSpec(memory_space=pl.ANY),
            vmem,
            vmem,
            vmem,
            pl.BlockSpec(memory_space=pltpu.SMEM),
        ],
        out_specs=vmem,
        scratch_shapes=[
            pltpu.VMEM((2, input_count, frames_dev), jnp.bfloat16),
            pltpu.VMEM((inp_size, 2, ranks, basis_lanes), jnp.float32),
            row_block,
            row_block,
            row_block,
            row_block,
            pltpu.VMEM((2 * ranks, input_count), jnp.bfloat16),
            weight,
            weight,
            pltpu.VMEM((inp_size, samples, beams_each), jnp.float32),
            pltpu.VMEM((inp_size, samples, beams_each), jnp.float32),
            dma,
            dma((devices,)),
            dma((devices,)),
            dma((inp_size,)),
            dma((inp_size,)),
            dma((inp_size,)),
            dma((inp_size,)),
        ],
        compiler_params=pltpu.CompilerParams(
            collective_id=0, has_side_effects=True, vmem_limit_bytes=40 * 1024 * 1024
        ),
    )(voltages, positions.T, directions.T, basis, rank_count)
    return jnp.transpose(result, (1, 0, 2))


def fits(mesh_sizes, voltages, positions, directions):
    inp_size, chan_size = mesh_sizes
    beams_each = directions.shape[0] // inp_size
    return (
        voltages.shape[2] % 16 == 0
        and (voltages.shape[3] // FGROUPS) % 128 == 0
        and positions.shape[0] % ROWS == 0
        and directions.shape[0] % ROWS == 0
        and ROWS % beams_each == 0
    )


def either(voltages, positions, directions, basis, rank_count):
    mesh_sizes = (lax.axis_size("inp"), lax.axis_size("chan"))
    way = fused if fits(mesh_sizes, voltages, positions, directions) else shards
    return way(voltages, positions, directions, basis, rank_count)


def solution(mesh):
    placed = (
        P(None, None, ("inp", "chan"), None),
        P(),
        P(),
        P(None, "chan", None, "inp"),
        P("chan"),
    )
    return jax.shard_map(
        either, mesh=mesh, in_specs=placed, out_specs=P("inp", "chan", None), check_vma=False
    )
```

```python
import functools
import math

import jax
import jax.numpy as jnp
import numpy as np
from jax import lax
from jax.experimental import pallas as pl
from jax.experimental.pallas import tpu as pltpu
from jax.sharding import PartitionSpec as P

FGROUPS = 8
DS = 16
ROWS = 128
FORM_ROWS = 256
MESH = pl.DeviceIdType.MESH


HIGHEST_PRECISION = lax.Precision.HIGHEST


def orthonormal(basis_rows, rank_used):
    ranks = basis_rows.shape[1]
    active = (jnp.arange(ranks) < rank_used).astype(basis_rows.dtype)

    def build_column(column_index, ortho_rows):
        real_part = lax.dynamic_index_in_dim(basis_rows[0], column_index, 0, keepdims=False)
        imag_part = lax.dynamic_index_in_dim(basis_rows[1], column_index, 0, keepdims=False)
        for second in range(2):
            coef_real = jnp.dot(ortho_rows[0], real_part, precision=HIGHEST_PRECISION) + jnp.dot(
                ortho_rows[1], imag_part, precision=HIGHEST_PRECISION
            )
            coef_imag = jnp.dot(ortho_rows[0], imag_part, precision=HIGHEST_PRECISION) - jnp.dot(
                ortho_rows[1], real_part, precision=HIGHEST_PRECISION
            )
            real_part = real_part - (
                jnp.dot(coef_real, ortho_rows[0], precision=HIGHEST_PRECISION)
                - jnp.dot(coef_imag, ortho_rows[1], precision=HIGHEST_PRECISION)
            )
            imag_part = imag_part - (
                jnp.dot(coef_real, ortho_rows[1], precision=HIGHEST_PRECISION)
                + jnp.dot(coef_imag, ortho_rows[0], precision=HIGHEST_PRECISION)
            )
        flag = lax.dynamic_index_in_dim(active, column_index, 0, keepdims=False)
        normalize = flag / jnp.sqrt(
            jnp.sum(real_part * real_part + imag_part * imag_part) + (1.0 - flag)
        )
        new_column = jnp.stack([real_part * normalize, imag_part * normalize])[:, None, :]
        return lax.dynamic_update_slice_in_dim(ortho_rows, new_column, column_index, 1)

    return lax.fori_loop(0, ranks, build_column, jnp.zeros_like(basis_rows))


def half_dot(left, right):
    return jnp.dot(left, right, preferred_element_type=jnp.float32)


def steer_block(row_start, row_count, positions, directions, ortho_rows, frequency):
    chosen = lax.dynamic_slice_in_dim(directions, row_start, row_count, 0)
    phase_angle = (
        2.0
        * jnp.pi
        * frequency
        * (chosen[:, 0:1] * positions[:, 0][None, :] + chosen[:, 1:2] * positions[:, 1][None, :])
    )
    inverse = 1.0 / math.sqrt(positions.shape[0])
    steer_real = jnp.cos(phase_angle) * inverse
    steer_imag = -jnp.sin(phase_angle) * inverse
    short_real = steer_real.astype(jnp.bfloat16)
    short_imag = steer_imag.astype(jnp.bfloat16)
    ortho_real = ortho_rows[0].astype(jnp.bfloat16)
    ortho_imag = ortho_rows[1].astype(jnp.bfloat16)
    along_real = (half_dot(short_real, ortho_real.T) - half_dot(short_imag, ortho_imag.T)).astype(
        jnp.bfloat16
    )
    along_imag = (half_dot(short_real, ortho_imag.T) + half_dot(short_imag, ortho_real.T)).astype(
        jnp.bfloat16
    )
    kept_real = steer_real - (half_dot(along_real, ortho_real) + half_dot(along_imag, ortho_imag))
    kept_imag = steer_imag - (half_dot(along_imag, ortho_real) - half_dot(along_real, ortho_imag))
    return (kept_real.astype(jnp.bfloat16), kept_imag.astype(jnp.bfloat16))


def projected_weights(positions, directions, ortho_rows, frequency):
    beam_count = directions.shape[0]
    row_count = min(beam_count, 512)
    block_count = beam_count // row_count

    def one_block(block_index):
        return steer_block(
            block_index * row_count, row_count, positions, directions, ortho_rows, frequency
        )

    weight_real, weight_imag = lax.map(one_block, jnp.arange(block_count, dtype=jnp.int32))
    input_count = positions.shape[0]
    return (
        weight_real.reshape(beam_count, input_count),
        weight_imag.reshape(beam_count, input_count),
    )


def detect(weight_real, weight_imag, volt_real, volt_imag):
    stacked = jnp.concatenate([volt_real, volt_imag], axis=1)
    frame_count = volt_real.shape[1]
    from_real = jnp.dot(weight_real, stacked, preferred_element_type=jnp.float32)
    from_imag = jnp.dot(weight_imag, stacked, preferred_element_type=jnp.float32)
    beam_real = from_real[:, :frame_count] - from_imag[:, frame_count:]
    beam_imag = from_real[:, frame_count:] + from_imag[:, :frame_count]
    return beam_real * beam_real + beam_imag * beam_imag


def shards(voltages, positions, directions, basis, rank_count):
    inp_size = lax.axis_size("inp")
    chan_size = lax.axis_size("chan")
    per_chan = inp_size // FGROUPS
    channels = chan_size * per_chan
    local_inputs = voltages.shape[2]
    frames_dev = voltages.shape[3] // FGROUPS
    input_count = positions.shape[0]
    beam_count = directions.shape[0]
    sub_channel = lax.axis_index("inp") // FGROUPS
    channel = lax.axis_index("chan") * per_chan + sub_channel
    frequency = 1.0 + 0.5 * channel.astype(jnp.float32) / channels
    rank_used = jnp.sum(jnp.where(jnp.arange(per_chan) == sub_channel, rank_count, 0))
    group_basis = lax.all_gather(basis, "inp", axis=3, tiled=True)
    own_basis = lax.dynamic_index_in_dim(group_basis, sub_channel, 1, keepdims=False)
    sectioned = voltages.reshape(2, chan_size, per_chan, local_inputs, FGROUPS, frames_dev)
    sectioned = jnp.transpose(sectioned, (0, 1, 2, 4, 3, 5)).reshape(
        2, chan_size, inp_size, local_inputs, frames_dev
    )
    ordered_positions = jnp.transpose(
        positions.reshape(inp_size, chan_size, local_inputs, 2), (1, 0, 2, 3)
    ).reshape(input_count, 2)
    ordered_basis = own_basis.reshape(2, own_basis.shape[1], inp_size, chan_size, local_inputs)
    ordered_basis = jnp.transpose(ordered_basis, (0, 1, 3, 2, 4)).reshape(
        2, own_basis.shape[1], input_count
    )
    ortho_rows = orthonormal(ordered_basis, rank_used)
    weight_real, weight_imag = projected_weights(
        ordered_positions, directions, ortho_rows, frequency
    )
    turned = lax.all_to_all(
        lax.all_to_all(sectioned, "inp", split_axis=2, concat_axis=3, tiled=True),
        "chan",
        split_axis=1,
        concat_axis=3,
        tiled=True,
    )
    detected = detect(weight_real, weight_imag, turned[0, 0, 0], turned[1, 0, 0])
    binned = jnp.mean(detected.reshape(beam_count, frames_dev // DS, DS), axis=2)
    regrouped = lax.all_to_all(binned[:, None, :], "inp", split_axis=0, concat_axis=1, tiled=True)
    return regrouped.reshape(beam_count // inp_size, per_chan, FGROUPS * (frames_dev // DS))


def turn_coefficients(input_count):
    nodes = np.cos(np.pi * (np.arange(400) + 0.5) / 400) * 0.25 * 0.5 + 0.125
    root = np.sqrt(nodes)
    scale = 1.0 / math.sqrt(input_count)
    fit = np.polynomial.chebyshev.Chebyshev.fit
    power = np.polynomial.Polynomial
    sin_fit = fit(nodes, np.sin(2 * np.pi * root) / root, 5, domain=[0, 0.25]).convert(kind=power)
    cos_fit = fit(nodes, np.cos(2 * np.pi * root), 6, domain=[0, 0.25]).convert(kind=power)
    return (
        [float(value) * scale for value in sin_fit.coef],
        [float(value) * scale for value in cos_fit.coef],
    )


def horner(coefs, x):
    total = jnp.full_like(x, coefs[-1])
    for value in coefs[-2::-1]:
        total = total * x + value
    return total


def across(left, right):
    return lax.dot_general(
        left, right, (((1,), (1,)), ((), ())), preferred_element_type=jnp.float32
    )


def fused_kernel(
    sizes,
    volt_ref,
    pos_hbm,
    dir_hbm,
    basis_hbm,
    rank_hbm,
    out_ref,
    pos_ref,
    dir_ref,
    basis_ref,
    rank_ref,
    turned,
    packed,
    basis_in,
    rows_real,
    rows_imag,
    ortho_real,
    ortho_imag,
    ortho_half,
    weight_real,
    weight_imag,
    power_out,
    power_in,
    local_sem,
    stage_sem,
    volt_send,
    volt_recv,
    basis_send,
    basis_recv,
    power_send,
    power_recv,
):
    inp_size, chan_size, per_chan, beam_count, frames_dev = sizes
    devices = inp_size * chan_size
    local_inputs = volt_ref.shape[2]
    input_count = pos_ref.shape[1]
    ranks = basis_ref.shape[2]
    my_inp = lax.axis_index("inp")
    my_chan = lax.axis_index("chan")
    me = my_inp * chan_size + my_chan
    sub = my_inp // FGROUPS
    samples = frames_dev // DS
    beams_each = beam_count // inp_size
    owners = FORM_ROWS // beams_each
    blocks = beam_count // ROWS
    form_blocks = beam_count // FORM_ROWS
    place = lax.rem(my_inp, FGROUPS)
    half = devices // per_chan

    def device(number):
        return (number // chan_size, lax.rem(number, chan_size))

    def other(k):
        return lax.rem(me + k, devices)

    def other_inp(k):
        return lax.rem(my_inp + k, inp_size)

    pairs = (
        (basis_hbm, basis_ref),
        (pos_hbm, pos_ref),
        (dir_hbm, dir_ref),
        (rank_hbm, rank_ref),
    )
    staged = [
        pltpu.make_async_copy(far, near, stage_sem.at[index])
        for index, (far, near) in enumerate(pairs)
    ]
    for copy in staged:
        copy.start()

    def spread(k):
        target_sub = lax.rem(sub + 1 + k // half, per_chan)
        return target_sub * half + lax.rem(me + k, half)

    barrier = pltpu.get_barrier_semaphore()

    def greet(k, carry):
        pl.semaphore_signal(barrier, inc=1, device_id=device(other(k)), device_id_type=MESH)
        return carry

    lax.fori_loop(1, devices, greet, 0)
    staged[0].wait()
    for index in range(per_chan):
        packed[index] = jnp.concatenate([basis_ref[0, index], basis_ref[1, index]], axis=1)
    basis_in[my_inp] = packed[sub]
    pl.semaphore_wait(barrier, devices - 1)

    def basis_cross(target_sub, slot):
        target = target_sub * FGROUPS + place
        return pltpu.make_async_remote_copy(
            src_ref=packed.at[target_sub],
            dst_ref=basis_in.at[slot],
            send_sem=basis_send.at[target],
            recv_sem=basis_recv.at[slot],
            device_id=(target, my_chan),
            device_id_type=MESH,
        )

    def basis_near(slot, peer):
        return pltpu.make_async_remote_copy(
            src_ref=basis_in.at[slot],
            dst_ref=basis_in.at[slot],
            send_sem=basis_send.at[slot // FGROUPS * FGROUPS + peer],
            recv_sem=basis_recv.at[slot],
            device_id=(sub * FGROUPS + peer, my_chan),
            device_id_type=MESH,
        )

    def peer(k):
        return lax.rem(place + k, FGROUPS)

    def volt_block(target):
        target_inp = target // chan_size
        channel = lax.rem(target, chan_size) * per_chan + target_inp // FGROUPS
        start = pl.multiple_of(lax.rem(target_inp, FGROUPS) * frames_dev, frames_dev)
        return volt_ref.at[:, channel, :, pl.ds(start, frames_dev)]

    def turned_block(slot):
        return turned.at[
            :, pl.ds(pl.multiple_of(slot * local_inputs, local_inputs), local_inputs), :
        ]

    def volt_copy(target, slot):
        return pltpu.make_async_remote_copy(
            src_ref=volt_block(target),
            dst_ref=turned_block(slot),
            send_sem=volt_send.at[target],
            recv_sem=volt_recv.at[slot],
            device_id=device(target),
            device_id_type=MESH,
        )

    def power_copy(target, slot):
        return pltpu.make_async_remote_copy(
            src_ref=power_out.at[target],
            dst_ref=power_in.at[slot],
            send_sem=power_send.at[target],
            recv_sem=power_recv.at[slot],
            device_id=(target, my_chan),
            device_id_type=MESH,
        )

    for offset in range(1, per_chan):
        basis_cross(lax.rem(sub + offset, per_chan), my_inp).start()

    def pass_basis(slot):
        def body(k, carry):
            basis_near(slot, peer(k)).start()
            return carry

        lax.fori_loop(1, FGROUPS, body, 0)

    pass_basis(my_inp)

    def send_volt(k, carry):
        volt_copy(spread(k), me).start()
        return carry

    lax.fori_loop(0, devices - half, send_volt, 0)
    for offset in range(1, per_chan):
        source = lax.rem(sub + offset, per_chan) * FGROUPS + place
        basis_near(source, place).wait_recv()
        pass_basis(source)
    lax.fori_loop(devices - half + 1, devices, send_volt, 0)
    own = pltpu.make_async_copy(volt_block(me), turned_block(me), local_sem)
    own.start()
    for copy in staged[1:]:
        copy.wait()

    def take_basis(index, carry):
        slot = index // (FGROUPS - 1) * FGROUPS + peer(lax.rem(index, FGROUPS - 1) + 1)
        basis_near(slot, place).wait_recv()
        return carry

    lax.fori_loop(0, per_chan * (FGROUPS - 1), take_basis, 0)
    lanes_each = basis_ref.shape[3]
    rows_real[...] = jnp.concatenate([basis_in[s, :, :lanes_each] for s in range(inp_size)], axis=1)
    rows_imag[...] = jnp.concatenate([basis_in[s, :, lanes_each:] for s in range(inp_size)], axis=1)
    ortho_real[...] = jnp.zeros_like(ortho_real)
    ortho_imag[...] = jnp.zeros_like(ortho_imag)
    rank_used = rank_ref[sub]

    def build_row(row, carry):
        real_part = rows_real[pl.ds(row, 1), :]
        imag_part = rows_imag[pl.ds(row, 1), :]
        for second in range(2):
            real_rows, imag_rows = ortho_real[...], ortho_imag[...]
            coef_real = jnp.sum(
                real_rows * real_part + imag_rows * imag_part, axis=1, keepdims=True
            )
            coef_imag = jnp.sum(
                real_rows * imag_part - imag_rows * real_part, axis=1, keepdims=True
            )
            real_part = real_part - jnp.sum(
                coef_real * real_rows - coef_imag * imag_rows, axis=0, keepdims=True
            )
            imag_part = imag_part - jnp.sum(
                coef_real * imag_rows + coef_imag * real_rows, axis=0, keepdims=True
            )
        flag = jnp.where(row < rank_used, 1.0, 0.0).astype(jnp.float32)
        square = jnp.sum(
            real_part * real_part + imag_part * imag_part, axis=1, keepdims=True
        )
        normalize = flag / jnp.sqrt(square + (1.0 - flag))
        ortho_real[pl.ds(row, 1), :] = real_part * normalize
        ortho_imag[pl.ds(row, 1), :] = imag_part * normalize
        return carry

    lax.fori_loop(0, ranks, build_row, 0)
    ortho_half[...] = jnp.concatenate([ortho_real[...], ortho_imag[...]], axis=0).astype(
        jnp.bfloat16
    )

    channel = my_chan * per_chan + sub
    frequency = 1.0 + 0.5 * channel.astype(jnp.float32) / (chan_size * per_chan)
    sin_coefs, cos_coefs = turn_coefficients(input_count)

    def weigh(block, carry):
        rows = pl.ds(pl.multiple_of(block * ROWS, ROWS), ROWS)
        first = jnp.broadcast_to(dir_ref[0:1, rows], (ROWS, ROWS)).T
        second = jnp.broadcast_to(dir_ref[1:2, rows], (ROWS, ROWS)).T
        reals, imags = [], []
        for piece in range(input_count // ROWS):
            lanes = slice(piece * ROWS, (piece + 1) * ROWS)
            turns = first * (pos_ref[0:1, lanes] * frequency) + second * (
                pos_ref[1:2, lanes] * frequency
            )
            turns = turns - jnp.round(turns)
            square = turns * turns
            reals.append(horner(cos_coefs, square))
            imags.append(-turns * horner(sin_coefs, square))
        steer_real = jnp.concatenate(reals, axis=1)
        steer_imag = jnp.concatenate(imags, axis=1)
        half = ortho_half[...]
        from_real = across(steer_real.astype(jnp.bfloat16), half)
        from_imag = across(steer_imag.astype(jnp.bfloat16), half)
        along_real = from_real[:, :ranks] - from_imag[:, ranks:]
        along_imag = from_real[:, ranks:] + from_imag[:, :ranks]
        for_real = jnp.concatenate([along_real, along_imag], axis=1).astype(jnp.bfloat16)
        for_imag = jnp.concatenate([along_imag, -along_real], axis=1).astype(jnp.bfloat16)
        weight_real[rows, :] = (steer_real - half_dot(for_real, half)).astype(jnp.bfloat16)
        weight_imag[rows, :] = (steer_imag - half_dot(for_imag, half)).astype(jnp.bfloat16)
        return carry

    lax.fori_loop(0, blocks, weigh, 0)

    def take_volt(k, carry):
        volt_copy(other(k), other(k)).wait_recv()
        return carry

    own.wait()
    lax.fori_loop(1, devices, take_volt, 0)

    sample_row = lax.broadcasted_iota(jnp.int32, (samples, frames_dev), 0)
    frame_column = lax.broadcasted_iota(jnp.int32, (samples, frames_dev), 1)
    inside = (frame_column >= sample_row * DS) & (frame_column < sample_row * DS + DS)
    pool = jnp.where(inside, 1.0 / DS, 0.0).astype(jnp.bfloat16)

    def form(step, carry):
        block = lax.rem(step + my_inp // owners, form_blocks)
        rows = pl.ds(pl.multiple_of(block * FORM_ROWS, FORM_ROWS), FORM_ROWS)
        volt_real, volt_imag = turned[0], turned[1]
        left, right = weight_real[rows, :], weight_imag[rows, :]
        beam_real = half_dot(left, volt_real) - half_dot(right, volt_imag)
        beam_imag = half_dot(left, volt_imag) + half_dot(right, volt_real)
        power = beam_real * beam_real + beam_imag * beam_imag
        high = power.astype(jnp.bfloat16)
        rest = power - high.astype(jnp.float32)
        middle = rest.astype(jnp.bfloat16)
        low = (rest - middle.astype(jnp.float32)).astype(jnp.bfloat16)
        binned = across(pool, high) + across(pool, middle) + across(pool, low)
        for part in range(owners):
            target = block * owners + part
            wide = binned[:, part * beams_each : (part + 1) * beams_each]
            piece = jnp.concatenate([wide[: samples // 2], wide[samples // 2 :]], axis=1)

            @pl.when(target == my_inp)
            def keep():
                power_in[my_inp] = piece

            @pl.when(target != my_inp)
            def pass_on():
                power_out[target] = piece
                power_copy(target, my_inp).start()

        return carry

    lax.fori_loop(0, form_blocks, form, 0)

    def take_power(k, carry):
        power_copy(other_inp(k), other_inp(k)).wait_recv()
        return carry

    lax.fori_loop(1, inp_size, take_power, 0)
    for index in range(per_chan):
        group = []
        for f in range(FGROUPS):
            piece = power_in[index * FGROUPS + f]
            group += [piece[:, :beams_each], piece[:, beams_each:]]
        out_ref[index] = jnp.concatenate(group, axis=0).T

    def finish_inp(k, carry):
        power_copy(other_inp(k), my_inp).wait_send()
        return carry

    lax.fori_loop(1, inp_size, finish_inp, 0)
    for offset in range(1, per_chan):
        basis_cross(lax.rem(sub + offset, per_chan), my_inp).wait_send()

    def finish_basis(index, carry):
        slot = index // (FGROUPS - 1) * FGROUPS + place
        basis_near(slot, peer(lax.rem(index, FGROUPS - 1) + 1)).wait_send()
        return carry

    lax.fori_loop(0, per_chan * (FGROUPS - 1), finish_basis, 0)

    def finish_volt(k, carry):
        volt_copy(other(k), me).wait_send()
        return carry

    lax.fori_loop(1, devices, finish_volt, 0)


def fused(voltages, positions, directions, basis, rank_count):
    inp_size = lax.axis_size("inp")
    chan_size = lax.axis_size("chan")
    devices = inp_size * chan_size
    per_chan = inp_size // FGROUPS
    frames_dev = voltages.shape[3] // FGROUPS
    input_count = positions.shape[0]
    beam_count = directions.shape[0]
    ranks = basis.shape[2]
    basis_lanes = basis.shape[3]
    samples = frames_dev // DS
    beams_each = beam_count // inp_size
    sizes = (inp_size, chan_size, per_chan, beam_count, frames_dev)
    vmem = pl.BlockSpec(memory_space=pltpu.VMEM)
    dma = pltpu.SemaphoreType.DMA
    row_block = pltpu.VMEM((ranks, input_count), jnp.float32)
    weight = pltpu.VMEM((beam_count, input_count), jnp.bfloat16)
    result = pl.pallas_call(
        functools.partial(fused_kernel, sizes),
        out_shape=jax.ShapeDtypeStruct(
            (per_chan, beams_each, FGROUPS * samples), jnp.float32
        ),
        in_specs=[pl.BlockSpec(memory_space=pl.ANY)] * 5,
        out_specs=vmem,
        scratch_shapes=[
            pltpu.VMEM((2, input_count), jnp.float32),
            pltpu.VMEM((2, beam_count), jnp.float32),
            pltpu.VMEM(basis.shape, jnp.float32),
            pltpu.SMEM(rank_count.shape, jnp.int32),
            pltpu.VMEM((2, input_count, frames_dev), jnp.bfloat16),
            pltpu.VMEM((per_chan, ranks, 2 * basis_lanes), jnp.float32),
            pltpu.VMEM((inp_size, ranks, 2 * basis_lanes), jnp.float32),
            row_block,
            row_block,
            row_block,
            row_block,
            pltpu.VMEM((2 * ranks, input_count), jnp.bfloat16),
            weight,
            weight,
            pltpu.VMEM((inp_size, samples // 2, 2 * beams_each), jnp.float32),
            pltpu.VMEM((inp_size, samples // 2, 2 * beams_each), jnp.float32),
            dma,
            dma((4,)),
            dma((devices,)),
            dma((devices,)),
            dma((inp_size,)),
            dma((inp_size,)),
            dma((inp_size,)),
            dma((inp_size,)),
        ],
        compiler_params=pltpu.CompilerParams(
            collective_id=0, has_side_effects=True, vmem_limit_bytes=60 * 1024 * 1024
        ),
    )(voltages, positions.T, directions.T, basis, rank_count)
    return jnp.transpose(result, (1, 0, 2))


def fits(mesh_sizes, voltages, positions, directions):
    inp_size, chan_size = mesh_sizes
    beams_each = directions.shape[0] // inp_size
    return (
        voltages.shape[2] % 16 == 0
        and (voltages.shape[3] // FGROUPS) % 128 == 0
        and positions.shape[0] % ROWS == 0
        and directions.shape[0] % FORM_ROWS == 0
        and FORM_ROWS % beams_each == 0
    )


def either(voltages, positions, directions, basis, rank_count):
    mesh_sizes = (lax.axis_size("inp"), lax.axis_size("chan"))
    way = fused if fits(mesh_sizes, voltages, positions, directions) else shards
    return way(voltages, positions, directions, basis, rank_count)


def solution(mesh):
    placed = (
        P(None, None, ("inp", "chan"), None),
        P(),
        P(),
        P(None, "chan", None, "inp"),
        P("chan"),
    )
    return jax.shard_map(
        either, mesh=mesh, in_specs=placed, out_specs=P("inp", "chan", None), check_vma=False
    )
```

```python
import functools
import math

import jax
import jax.numpy as jnp
import numpy as np
from jax import lax
from jax.experimental import pallas as pl
from jax.experimental.pallas import tpu as pltpu
from jax.sharding import PartitionSpec as P

FGROUPS = 8
DS = 16
ROWS = 128
FORM_ROWS = 256
FIRST_SENDS = 2
MESH = pl.DeviceIdType.MESH


HIGHEST_PRECISION = lax.Precision.HIGHEST


def orthonormal(basis_rows, rank_used):
    ranks = basis_rows.shape[1]
    active = (jnp.arange(ranks) < rank_used).astype(basis_rows.dtype)

    def build_column(column_index, ortho_rows):
        real_part = lax.dynamic_index_in_dim(basis_rows[0], column_index, 0, keepdims=False)
        imag_part = lax.dynamic_index_in_dim(basis_rows[1], column_index, 0, keepdims=False)
        for second in range(2):
            coef_real = jnp.dot(ortho_rows[0], real_part, precision=HIGHEST_PRECISION) + jnp.dot(
                ortho_rows[1], imag_part, precision=HIGHEST_PRECISION
            )
            coef_imag = jnp.dot(ortho_rows[0], imag_part, precision=HIGHEST_PRECISION) - jnp.dot(
                ortho_rows[1], real_part, precision=HIGHEST_PRECISION
            )
            real_part = real_part - (
                jnp.dot(coef_real, ortho_rows[0], precision=HIGHEST_PRECISION)
                - jnp.dot(coef_imag, ortho_rows[1], precision=HIGHEST_PRECISION)
            )
            imag_part = imag_part - (
                jnp.dot(coef_real, ortho_rows[1], precision=HIGHEST_PRECISION)
                + jnp.dot(coef_imag, ortho_rows[0], precision=HIGHEST_PRECISION)
            )
        flag = lax.dynamic_index_in_dim(active, column_index, 0, keepdims=False)
        normalize = flag / jnp.sqrt(
            jnp.sum(real_part * real_part + imag_part * imag_part) + (1.0 - flag)
        )
        new_column = jnp.stack([real_part * normalize, imag_part * normalize])[:, None, :]
        return lax.dynamic_update_slice_in_dim(ortho_rows, new_column, column_index, 1)

    return lax.fori_loop(0, ranks, build_column, jnp.zeros_like(basis_rows))


def half_dot(left, right):
    return jnp.dot(left, right, preferred_element_type=jnp.float32)


def steer_block(row_start, row_count, positions, directions, ortho_rows, frequency):
    chosen = lax.dynamic_slice_in_dim(directions, row_start, row_count, 0)
    phase_angle = (
        2.0
        * jnp.pi
        * frequency
        * (chosen[:, 0:1] * positions[:, 0][None, :] + chosen[:, 1:2] * positions[:, 1][None, :])
    )
    inverse = 1.0 / math.sqrt(positions.shape[0])
    steer_real = jnp.cos(phase_angle) * inverse
    steer_imag = -jnp.sin(phase_angle) * inverse
    short_real = steer_real.astype(jnp.bfloat16)
    short_imag = steer_imag.astype(jnp.bfloat16)
    ortho_real = ortho_rows[0].astype(jnp.bfloat16)
    ortho_imag = ortho_rows[1].astype(jnp.bfloat16)
    along_real = (half_dot(short_real, ortho_real.T) - half_dot(short_imag, ortho_imag.T)).astype(
        jnp.bfloat16
    )
    along_imag = (half_dot(short_real, ortho_imag.T) + half_dot(short_imag, ortho_real.T)).astype(
        jnp.bfloat16
    )
    kept_real = steer_real - (half_dot(along_real, ortho_real) + half_dot(along_imag, ortho_imag))
    kept_imag = steer_imag - (half_dot(along_imag, ortho_real) - half_dot(along_real, ortho_imag))
    return (kept_real.astype(jnp.bfloat16), kept_imag.astype(jnp.bfloat16))


def projected_weights(positions, directions, ortho_rows, frequency):
    beam_count = directions.shape[0]
    row_count = min(beam_count, 512)
    block_count = beam_count // row_count

    def one_block(block_index):
        return steer_block(
            block_index * row_count, row_count, positions, directions, ortho_rows, frequency
        )

    weight_real, weight_imag = lax.map(one_block, jnp.arange(block_count, dtype=jnp.int32))
    input_count = positions.shape[0]
    return (
        weight_real.reshape(beam_count, input_count),
        weight_imag.reshape(beam_count, input_count),
    )


def detect(weight_real, weight_imag, volt_real, volt_imag):
    stacked = jnp.concatenate([volt_real, volt_imag], axis=1)
    frame_count = volt_real.shape[1]
    from_real = jnp.dot(weight_real, stacked, preferred_element_type=jnp.float32)
    from_imag = jnp.dot(weight_imag, stacked, preferred_element_type=jnp.float32)
    beam_real = from_real[:, :frame_count] - from_imag[:, frame_count:]
    beam_imag = from_real[:, frame_count:] + from_imag[:, :frame_count]
    return beam_real * beam_real + beam_imag * beam_imag


def shards(voltages, positions, directions, basis, rank_count):
    inp_size = lax.axis_size("inp")
    chan_size = lax.axis_size("chan")
    per_chan = inp_size // FGROUPS
    channels = chan_size * per_chan
    local_inputs = voltages.shape[2]
    frames_dev = voltages.shape[3] // FGROUPS
    input_count = positions.shape[0]
    beam_count = directions.shape[0]
    sub_channel = lax.axis_index("inp") // FGROUPS
    channel = lax.axis_index("chan") * per_chan + sub_channel
    frequency = 1.0 + 0.5 * channel.astype(jnp.float32) / channels
    rank_used = jnp.sum(jnp.where(jnp.arange(per_chan) == sub_channel, rank_count, 0))
    group_basis = lax.all_gather(basis, "inp", axis=3, tiled=True)
    own_basis = lax.dynamic_index_in_dim(group_basis, sub_channel, 1, keepdims=False)
    sectioned = voltages.reshape(2, chan_size, per_chan, local_inputs, FGROUPS, frames_dev)
    sectioned = jnp.transpose(sectioned, (0, 1, 2, 4, 3, 5)).reshape(
        2, chan_size, inp_size, local_inputs, frames_dev
    )
    ordered_positions = jnp.transpose(
        positions.reshape(inp_size, chan_size, local_inputs, 2), (1, 0, 2, 3)
    ).reshape(input_count, 2)
    ordered_basis = own_basis.reshape(2, own_basis.shape[1], inp_size, chan_size, local_inputs)
    ordered_basis = jnp.transpose(ordered_basis, (0, 1, 3, 2, 4)).reshape(
        2, own_basis.shape[1], input_count
    )
    ortho_rows = orthonormal(ordered_basis, rank_used)
    weight_real, weight_imag = projected_weights(
        ordered_positions, directions, ortho_rows, frequency
    )
    turned = lax.all_to_all(
        lax.all_to_all(sectioned, "inp", split_axis=2, concat_axis=3, tiled=True),
        "chan",
        split_axis=1,
        concat_axis=3,
        tiled=True,
    )
    detected = detect(weight_real, weight_imag, turned[0, 0, 0], turned[1, 0, 0])
    binned = jnp.mean(detected.reshape(beam_count, frames_dev // DS, DS), axis=2)
    regrouped = lax.all_to_all(binned[:, None, :], "inp", split_axis=0, concat_axis=1, tiled=True)
    return regrouped.reshape(beam_count // inp_size, per_chan, FGROUPS * (frames_dev // DS))


def turn_coefficients(input_count):
    nodes = np.cos(np.pi * (np.arange(400) + 0.5) / 400) * 0.25 * 0.5 + 0.125
    root = np.sqrt(nodes)
    scale = 1.0 / math.sqrt(input_count)
    fit = np.polynomial.chebyshev.Chebyshev.fit
    power = np.polynomial.Polynomial
    sin_fit = fit(nodes, np.sin(2 * np.pi * root) / root, 5, domain=[0, 0.25]).convert(kind=power)
    cos_fit = fit(nodes, np.cos(2 * np.pi * root), 6, domain=[0, 0.25]).convert(kind=power)
    return (
        [float(value) * scale for value in sin_fit.coef],
        [float(value) * scale for value in cos_fit.coef],
    )


def horner(coefs, x):
    total = jnp.full_like(x, coefs[-1])
    for value in coefs[-2::-1]:
        total = total * x + value
    return total


def across(left, right):
    return lax.dot_general(
        left, right, (((1,), (1,)), ((), ())), preferred_element_type=jnp.float32
    )


def fused_kernel(
    sizes,
    volt_ref,
    pos_hbm,
    dir_hbm,
    basis_hbm,
    rank_hbm,
    out_ref,
    pos_ref,
    dir_ref,
    basis_ref,
    rank_ref,
    turned,
    packed,
    basis_in,
    rows_real,
    rows_imag,
    ortho_real,
    ortho_imag,
    ortho_half,
    steer_real,
    steer_imag,
    weight_real,
    weight_imag,
    power_out,
    power_in,
    local_sem,
    stage_sem,
    volt_send,
    volt_recv,
    basis_send,
    basis_recv,
    power_send,
    power_recv,
):
    inp_size, chan_size, per_chan, beam_count, frames_dev = sizes
    devices = inp_size * chan_size
    local_inputs = volt_ref.shape[2]
    input_count = pos_ref.shape[1]
    ranks = basis_ref.shape[2]
    my_inp = lax.axis_index("inp")
    my_chan = lax.axis_index("chan")
    me = my_inp * chan_size + my_chan
    sub = my_inp // FGROUPS
    samples = frames_dev // DS
    beams_each = beam_count // inp_size
    owners = FORM_ROWS // beams_each
    blocks = beam_count // ROWS
    form_blocks = beam_count // FORM_ROWS
    place = lax.rem(my_inp, FGROUPS)
    half = devices // per_chan

    def device(number):
        return (number // chan_size, lax.rem(number, chan_size))

    def other(k):
        return lax.rem(me + k, devices)

    def other_inp(k):
        return lax.rem(my_inp + k, inp_size)

    pairs = (
        (basis_hbm, basis_ref),
        (pos_hbm, pos_ref),
        (dir_hbm, dir_ref),
        (rank_hbm, rank_ref),
    )
    staged = [
        pltpu.make_async_copy(far, near, stage_sem.at[index])
        for index, (far, near) in enumerate(pairs)
    ]
    for copy in staged:
        copy.start()

    def spread(k):
        target_sub = lax.rem(sub + 1 + k // half, per_chan)
        return target_sub * half + lax.rem(me + k, half)

    barrier = pltpu.get_barrier_semaphore()

    def greet(k, carry):
        pl.semaphore_signal(barrier, inc=1, device_id=device(other(k)), device_id_type=MESH)
        return carry

    lax.fori_loop(1, devices, greet, 0)
    staged[0].wait()
    for index in range(per_chan):
        packed[index] = jnp.concatenate([basis_ref[0, index], basis_ref[1, index]], axis=1)
    basis_in[my_inp] = packed[sub]
    pl.semaphore_wait(barrier, devices - 1)

    def basis_cross(target_sub, slot):
        target = target_sub * FGROUPS + place
        return pltpu.make_async_remote_copy(
            src_ref=packed.at[target_sub],
            dst_ref=basis_in.at[slot],
            send_sem=basis_send.at[target],
            recv_sem=basis_recv.at[slot],
            device_id=(target, my_chan),
            device_id_type=MESH,
        )

    def basis_near(slot, peer):
        return pltpu.make_async_remote_copy(
            src_ref=basis_in.at[slot],
            dst_ref=basis_in.at[slot],
            send_sem=basis_send.at[slot // FGROUPS * FGROUPS + peer],
            recv_sem=basis_recv.at[slot],
            device_id=(sub * FGROUPS + peer, my_chan),
            device_id_type=MESH,
        )

    def peer(k):
        return lax.rem(place + k, FGROUPS)

    def volt_block(target):
        target_inp = target // chan_size
        channel = lax.rem(target, chan_size) * per_chan + target_inp // FGROUPS
        start = pl.multiple_of(lax.rem(target_inp, FGROUPS) * frames_dev, frames_dev)
        return volt_ref.at[:, channel, :, pl.ds(start, frames_dev)]

    def turned_block(slot):
        return turned.at[
            :, pl.ds(pl.multiple_of(slot * local_inputs, local_inputs), local_inputs), :
        ]

    def volt_copy(target, slot):
        return pltpu.make_async_remote_copy(
            src_ref=volt_block(target),
            dst_ref=turned_block(slot),
            send_sem=volt_send.at[target],
            recv_sem=volt_recv.at[slot],
            device_id=device(target),
            device_id_type=MESH,
        )

    def power_copy(target, slot):
        return pltpu.make_async_remote_copy(
            src_ref=power_out.at[target],
            dst_ref=power_in.at[slot],
            send_sem=power_send.at[target],
            recv_sem=power_recv.at[slot],
            device_id=(target, my_chan),
            device_id_type=MESH,
        )

    for offset in range(1, per_chan):
        basis_cross(lax.rem(sub + offset, per_chan), my_inp).start()

    def pass_basis(slot):
        def body(k, carry):
            basis_near(slot, peer(k)).start()
            return carry

        lax.fori_loop(1, FGROUPS, body, 0)

    pass_basis(my_inp)

    def send_volt(k, carry):
        volt_copy(spread(k), me).start()
        return carry

    lax.fori_loop(0, FIRST_SENDS, send_volt, 0)
    for offset in range(1, per_chan):
        source = lax.rem(sub + offset, per_chan) * FGROUPS + place
        basis_near(source, place).wait_recv()
        pass_basis(source)
    lax.fori_loop(FIRST_SENDS, devices - half, send_volt, 0)
    lax.fori_loop(devices - half + 1, devices, send_volt, 0)
    own = pltpu.make_async_copy(volt_block(me), turned_block(me), local_sem)
    own.start()
    for copy in staged[1:]:
        copy.wait()

    channel = my_chan * per_chan + sub
    frequency = 1.0 + 0.5 * channel.astype(jnp.float32) / (chan_size * per_chan)
    sin_coefs, cos_coefs = turn_coefficients(input_count)

    def steer(block, carry):
        rows = pl.ds(pl.multiple_of(block * ROWS, ROWS), ROWS)
        first = jnp.broadcast_to(dir_ref[0:1, rows], (ROWS, ROWS)).T
        second = jnp.broadcast_to(dir_ref[1:2, rows], (ROWS, ROWS)).T
        for piece in range(input_count // ROWS):
            lanes = slice(piece * ROWS, (piece + 1) * ROWS)
            turns = first * (pos_ref[0:1, lanes] * frequency) + second * (
                pos_ref[1:2, lanes] * frequency
            )
            turns = turns - jnp.round(turns)
            square = turns * turns
            steer_real[rows, lanes] = horner(cos_coefs, square)
            steer_imag[rows, lanes] = -turns * horner(sin_coefs, square)
        return carry

    lax.fori_loop(0, blocks, steer, 0)

    def take_basis(index, carry):
        slot = index // (FGROUPS - 1) * FGROUPS + peer(lax.rem(index, FGROUPS - 1) + 1)
        basis_near(slot, place).wait_recv()
        return carry

    lax.fori_loop(0, per_chan * (FGROUPS - 1), take_basis, 0)
    lanes_each = basis_ref.shape[3]
    rows_real[...] = jnp.concatenate([basis_in[s, :, :lanes_each] for s in range(inp_size)], axis=1)
    rows_imag[...] = jnp.concatenate([basis_in[s, :, lanes_each:] for s in range(inp_size)], axis=1)
    ortho_real[...] = jnp.zeros_like(ortho_real)
    ortho_imag[...] = jnp.zeros_like(ortho_imag)
    rank_used = rank_ref[sub]

    def build_row(row, carry):
        real_part = rows_real[pl.ds(row, 1), :]
        imag_part = rows_imag[pl.ds(row, 1), :]
        for second in range(2):
            real_rows, imag_rows = ortho_real[...], ortho_imag[...]
            coef_real = jnp.sum(
                real_rows * real_part + imag_rows * imag_part, axis=1, keepdims=True
            )
            coef_imag = jnp.sum(
                real_rows * imag_part - imag_rows * real_part, axis=1, keepdims=True
            )
            real_part = real_part - jnp.sum(
                coef_real * real_rows - coef_imag * imag_rows, axis=0, keepdims=True
            )
            imag_part = imag_part - jnp.sum(
                coef_real * imag_rows + coef_imag * real_rows, axis=0, keepdims=True
            )
        flag = jnp.where(row < rank_used, 1.0, 0.0).astype(jnp.float32)
        square = jnp.sum(
            real_part * real_part + imag_part * imag_part, axis=1, keepdims=True
        )
        normalize = flag / jnp.sqrt(square + (1.0 - flag))
        ortho_real[pl.ds(row, 1), :] = real_part * normalize
        ortho_imag[pl.ds(row, 1), :] = imag_part * normalize
        return carry

    lax.fori_loop(0, ranks, build_row, 0)
    ortho_half[...] = jnp.concatenate([ortho_real[...], ortho_imag[...]], axis=0).astype(
        jnp.bfloat16
    )

    def project(block, carry):
        rows = pl.ds(pl.multiple_of(block * FORM_ROWS, FORM_ROWS), FORM_ROWS)
        half_rows = ortho_half[...]
        from_real = across(steer_real[rows, :].astype(jnp.bfloat16), half_rows)
        from_imag = across(steer_imag[rows, :].astype(jnp.bfloat16), half_rows)
        along_real = from_real[:, :ranks] - from_imag[:, ranks:]
        along_imag = from_real[:, ranks:] + from_imag[:, :ranks]
        for_real = jnp.concatenate([along_real, along_imag], axis=1).astype(jnp.bfloat16)
        for_imag = jnp.concatenate([along_imag, -along_real], axis=1).astype(jnp.bfloat16)
        weight_real[rows, :] = (steer_real[rows, :] - half_dot(for_real, half_rows)).astype(
            jnp.bfloat16
        )
        weight_imag[rows, :] = (steer_imag[rows, :] - half_dot(for_imag, half_rows)).astype(
            jnp.bfloat16
        )
        return carry

    lax.fori_loop(0, form_blocks, project, 0)

    def take_volt(k, carry):
        volt_copy(other(k), other(k)).wait_recv()
        return carry

    own.wait()
    lax.fori_loop(1, devices, take_volt, 0)

    sample_row = lax.broadcasted_iota(jnp.int32, (samples, frames_dev), 0)
    frame_column = lax.broadcasted_iota(jnp.int32, (samples, frames_dev), 1)
    inside = (frame_column >= sample_row * DS) & (frame_column < sample_row * DS + DS)
    pool = jnp.where(inside, 1.0 / DS, 0.0).astype(jnp.bfloat16)

    def form(step, carry):
        block = lax.rem(step + my_inp // owners + 1, form_blocks)
        rows = pl.ds(pl.multiple_of(block * FORM_ROWS, FORM_ROWS), FORM_ROWS)
        volt_real, volt_imag = turned[0], turned[1]
        left, right = weight_real[rows, :], weight_imag[rows, :]
        beam_real = half_dot(left, volt_real) - half_dot(right, volt_imag)
        beam_imag = half_dot(left, volt_imag) + half_dot(right, volt_real)
        power = beam_real * beam_real + beam_imag * beam_imag
        high = power.astype(jnp.bfloat16)
        rest = power - high.astype(jnp.float32)
        middle = rest.astype(jnp.bfloat16)
        low = (rest - middle.astype(jnp.float32)).astype(jnp.bfloat16)
        binned = across(pool, high) + across(pool, middle) + across(pool, low)
        for part in range(owners):
            target = block * owners + part
            wide = binned[:, part * beams_each : (part + 1) * beams_each]
            piece = jnp.concatenate([wide[: samples // 2], wide[samples // 2 :]], axis=1)

            @pl.when(target == my_inp)
            def keep():
                power_in[my_inp] = piece

            @pl.when(target != my_inp)
            def pass_on():
                power_out[target] = piece
                power_copy(target, my_inp).start()

        return carry

    lax.fori_loop(0, form_blocks, form, 0)

    def take_power(k, carry):
        power_copy(other_inp(k), other_inp(k)).wait_recv()
        return carry

    lax.fori_loop(1, inp_size, take_power, 0)
    for index in range(per_chan):
        group = []
        for f in range(FGROUPS):
            piece = power_in[index * FGROUPS + f]
            group += [piece[:, :beams_each], piece[:, beams_each:]]
        out_ref[index] = jnp.concatenate(group, axis=0).T

    def finish_inp(k, carry):
        power_copy(other_inp(k), my_inp).wait_send()
        return carry

    lax.fori_loop(1, inp_size, finish_inp, 0)
    for offset in range(1, per_chan):
        basis_cross(lax.rem(sub + offset, per_chan), my_inp).wait_send()

    def finish_basis(index, carry):
        slot = index // (FGROUPS - 1) * FGROUPS + place
        basis_near(slot, peer(lax.rem(index, FGROUPS - 1) + 1)).wait_send()
        return carry

    lax.fori_loop(0, per_chan * (FGROUPS - 1), finish_basis, 0)

    def finish_volt(k, carry):
        volt_copy(other(k), me).wait_send()
        return carry

    lax.fori_loop(1, devices, finish_volt, 0)


def fused(voltages, positions, directions, basis, rank_count):
    inp_size = lax.axis_size("inp")
    chan_size = lax.axis_size("chan")
    devices = inp_size * chan_size
    per_chan = inp_size // FGROUPS
    frames_dev = voltages.shape[3] // FGROUPS
    input_count = positions.shape[0]
    beam_count = directions.shape[0]
    ranks = basis.shape[2]
    basis_lanes = basis.shape[3]
    samples = frames_dev // DS
    beams_each = beam_count // inp_size
    sizes = (inp_size, chan_size, per_chan, beam_count, frames_dev)
    vmem = pl.BlockSpec(memory_space=pltpu.VMEM)
    dma = pltpu.SemaphoreType.DMA
    row_block = pltpu.VMEM((ranks, input_count), jnp.float32)
    weight = pltpu.VMEM((beam_count, input_count), jnp.bfloat16)
    wave = pltpu.VMEM((beam_count, input_count), jnp.float32)
    result = pl.pallas_call(
        functools.partial(fused_kernel, sizes),
        out_shape=jax.ShapeDtypeStruct(
            (per_chan, beams_each, FGROUPS * samples), jnp.float32
        ),
        in_specs=[pl.BlockSpec(memory_space=pl.ANY)] * 5,
        out_specs=vmem,
        scratch_shapes=[
            pltpu.VMEM((2, input_count), jnp.float32),
            pltpu.VMEM((2, beam_count), jnp.float32),
            pltpu.VMEM(basis.shape, jnp.float32),
            pltpu.SMEM(rank_count.shape, jnp.int32),
            pltpu.VMEM((2, input_count, frames_dev), jnp.bfloat16),
            pltpu.VMEM((per_chan, ranks, 2 * basis_lanes), jnp.float32),
            pltpu.VMEM((inp_size, ranks, 2 * basis_lanes), jnp.float32),
            row_block,
            row_block,
            row_block,
            row_block,
            pltpu.VMEM((2 * ranks, input_count), jnp.bfloat16),
            wave,
            wave,
            weight,
            weight,
            pltpu.VMEM((inp_size, samples // 2, 2 * beams_each), jnp.float32),
            pltpu.VMEM((inp_size, samples // 2, 2 * beams_each), jnp.float32),
            dma,
            dma((4,)),
            dma((devices,)),
            dma((devices,)),
            dma((inp_size,)),
            dma((inp_size,)),
            dma((inp_size,)),
            dma((inp_size,)),
        ],
        compiler_params=pltpu.CompilerParams(
            collective_id=0, has_side_effects=True, vmem_limit_bytes=60 * 1024 * 1024
        ),
    )(voltages, positions.T, directions.T, basis, rank_count)
    return jnp.transpose(result, (1, 0, 2))


def fits(mesh_sizes, voltages, positions, directions):
    inp_size, chan_size = mesh_sizes
    beams_each = directions.shape[0] // inp_size
    return (
        voltages.shape[2] % 16 == 0
        and (voltages.shape[3] // FGROUPS) % 128 == 0
        and positions.shape[0] % ROWS == 0
        and directions.shape[0] % FORM_ROWS == 0
        and FORM_ROWS % beams_each == 0
    )


def either(voltages, positions, directions, basis, rank_count):
    mesh_sizes = (lax.axis_size("inp"), lax.axis_size("chan"))
    way = fused if fits(mesh_sizes, voltages, positions, directions) else shards
    return way(voltages, positions, directions, basis, rank_count)


def solution(mesh):
    placed = (
        P(None, None, ("inp", "chan"), None),
        P(),
        P(),
        P(None, "chan", None, "inp"),
        P("chan"),
    )
    return jax.shard_map(
        either, mesh=mesh, in_specs=placed, out_specs=P("inp", "chan", None), check_vma=False
    )
```

```python
import functools
import math

import jax
import jax.numpy as jnp
import numpy as np
from jax import lax
from jax.experimental import pallas as pl
from jax.experimental.pallas import tpu as pltpu
from jax.sharding import PartitionSpec as P

FGROUPS = 8
DS = 16
ROWS = 128
FORM_ROWS = 256
FIRST_SENDS = 2
MESH = pl.DeviceIdType.MESH


HIGHEST_PRECISION = lax.Precision.HIGHEST


def orthonormal(basis_rows, rank_used):
    ranks = basis_rows.shape[1]
    active = (jnp.arange(ranks) < rank_used).astype(basis_rows.dtype)

    def build_column(column_index, ortho_rows):
        real_part = lax.dynamic_index_in_dim(basis_rows[0], column_index, 0, keepdims=False)
        imag_part = lax.dynamic_index_in_dim(basis_rows[1], column_index, 0, keepdims=False)
        for second in range(2):
            coef_real = jnp.dot(ortho_rows[0], real_part, precision=HIGHEST_PRECISION) + jnp.dot(
                ortho_rows[1], imag_part, precision=HIGHEST_PRECISION
            )
            coef_imag = jnp.dot(ortho_rows[0], imag_part, precision=HIGHEST_PRECISION) - jnp.dot(
                ortho_rows[1], real_part, precision=HIGHEST_PRECISION
            )
            real_part = real_part - (
                jnp.dot(coef_real, ortho_rows[0], precision=HIGHEST_PRECISION)
                - jnp.dot(coef_imag, ortho_rows[1], precision=HIGHEST_PRECISION)
            )
            imag_part = imag_part - (
                jnp.dot(coef_real, ortho_rows[1], precision=HIGHEST_PRECISION)
                + jnp.dot(coef_imag, ortho_rows[0], precision=HIGHEST_PRECISION)
            )
        flag = lax.dynamic_index_in_dim(active, column_index, 0, keepdims=False)
        normalize = flag / jnp.sqrt(
            jnp.sum(real_part * real_part + imag_part * imag_part) + (1.0 - flag)
        )
        new_column = jnp.stack([real_part * normalize, imag_part * normalize])[:, None, :]
        return lax.dynamic_update_slice_in_dim(ortho_rows, new_column, column_index, 1)

    return lax.fori_loop(0, ranks, build_column, jnp.zeros_like(basis_rows))


def half_dot(left, right):
    return jnp.dot(left, right, preferred_element_type=jnp.float32)


def steer_block(row_start, row_count, positions, directions, ortho_rows, frequency):
    chosen = lax.dynamic_slice_in_dim(directions, row_start, row_count, 0)
    phase_angle = (
        2.0
        * jnp.pi
        * frequency
        * (chosen[:, 0:1] * positions[:, 0][None, :] + chosen[:, 1:2] * positions[:, 1][None, :])
    )
    inverse = 1.0 / math.sqrt(positions.shape[0])
    steer_real = jnp.cos(phase_angle) * inverse
    steer_imag = -jnp.sin(phase_angle) * inverse
    short_real = steer_real.astype(jnp.bfloat16)
    short_imag = steer_imag.astype(jnp.bfloat16)
    ortho_real = ortho_rows[0].astype(jnp.bfloat16)
    ortho_imag = ortho_rows[1].astype(jnp.bfloat16)
    along_real = (half_dot(short_real, ortho_real.T) - half_dot(short_imag, ortho_imag.T)).astype(
        jnp.bfloat16
    )
    along_imag = (half_dot(short_real, ortho_imag.T) + half_dot(short_imag, ortho_real.T)).astype(
        jnp.bfloat16
    )
    kept_real = steer_real - (half_dot(along_real, ortho_real) + half_dot(along_imag, ortho_imag))
    kept_imag = steer_imag - (half_dot(along_imag, ortho_real) - half_dot(along_real, ortho_imag))
    return (kept_real.astype(jnp.bfloat16), kept_imag.astype(jnp.bfloat16))


def projected_weights(positions, directions, ortho_rows, frequency):
    beam_count = directions.shape[0]
    row_count = min(beam_count, 512)
    block_count = beam_count // row_count

    def one_block(block_index):
        return steer_block(
            block_index * row_count, row_count, positions, directions, ortho_rows, frequency
        )

    weight_real, weight_imag = lax.map(one_block, jnp.arange(block_count, dtype=jnp.int32))
    input_count = positions.shape[0]
    return (
        weight_real.reshape(beam_count, input_count),
        weight_imag.reshape(beam_count, input_count),
    )


def detect(weight_real, weight_imag, volt_real, volt_imag):
    stacked = jnp.concatenate([volt_real, volt_imag], axis=1)
    frame_count = volt_real.shape[1]
    from_real = jnp.dot(weight_real, stacked, preferred_element_type=jnp.float32)
    from_imag = jnp.dot(weight_imag, stacked, preferred_element_type=jnp.float32)
    beam_real = from_real[:, :frame_count] - from_imag[:, frame_count:]
    beam_imag = from_real[:, frame_count:] + from_imag[:, :frame_count]
    return beam_real * beam_real + beam_imag * beam_imag


def shards(voltages, positions, directions, basis, rank_count):
    inp_size = lax.axis_size("inp")
    chan_size = lax.axis_size("chan")
    per_chan = inp_size // FGROUPS
    channels = chan_size * per_chan
    local_inputs = voltages.shape[2]
    frames_dev = voltages.shape[3] // FGROUPS
    input_count = positions.shape[0]
    beam_count = directions.shape[0]
    sub_channel = lax.axis_index("inp") // FGROUPS
    channel = lax.axis_index("chan") * per_chan + sub_channel
    frequency = 1.0 + 0.5 * channel.astype(jnp.float32) / channels
    rank_used = jnp.sum(jnp.where(jnp.arange(per_chan) == sub_channel, rank_count, 0))
    group_basis = lax.all_gather(basis, "inp", axis=3, tiled=True)
    own_basis = lax.dynamic_index_in_dim(group_basis, sub_channel, 1, keepdims=False)
    sectioned = voltages.reshape(2, chan_size, per_chan, local_inputs, FGROUPS, frames_dev)
    sectioned = jnp.transpose(sectioned, (0, 1, 2, 4, 3, 5)).reshape(
        2, chan_size, inp_size, local_inputs, frames_dev
    )
    ordered_positions = jnp.transpose(
        positions.reshape(inp_size, chan_size, local_inputs, 2), (1, 0, 2, 3)
    ).reshape(input_count, 2)
    ordered_basis = own_basis.reshape(2, own_basis.shape[1], inp_size, chan_size, local_inputs)
    ordered_basis = jnp.transpose(ordered_basis, (0, 1, 3, 2, 4)).reshape(
        2, own_basis.shape[1], input_count
    )
    ortho_rows = orthonormal(ordered_basis, rank_used)
    weight_real, weight_imag = projected_weights(
        ordered_positions, directions, ortho_rows, frequency
    )
    turned = lax.all_to_all(
        lax.all_to_all(sectioned, "inp", split_axis=2, concat_axis=3, tiled=True),
        "chan",
        split_axis=1,
        concat_axis=3,
        tiled=True,
    )
    detected = detect(weight_real, weight_imag, turned[0, 0, 0], turned[1, 0, 0])
    binned = jnp.mean(detected.reshape(beam_count, frames_dev // DS, DS), axis=2)
    regrouped = lax.all_to_all(binned[:, None, :], "inp", split_axis=0, concat_axis=1, tiled=True)
    return regrouped.reshape(beam_count // inp_size, per_chan, FGROUPS * (frames_dev // DS))


def turn_coefficients(input_count):
    nodes = np.cos(np.pi * (np.arange(400) + 0.5) / 400) * 0.25 * 0.5 + 0.125
    root = np.sqrt(nodes)
    scale = 1.0 / math.sqrt(input_count)
    fit = np.polynomial.chebyshev.Chebyshev.fit
    power = np.polynomial.Polynomial
    sin_fit = fit(nodes, np.sin(2 * np.pi * root) / root, 5, domain=[0, 0.25]).convert(kind=power)
    cos_fit = fit(nodes, np.cos(2 * np.pi * root), 6, domain=[0, 0.25]).convert(kind=power)
    return (
        [float(value) * scale for value in sin_fit.coef],
        [float(value) * scale for value in cos_fit.coef],
    )


def horner(coefs, x):
    total = jnp.full_like(x, coefs[-1])
    for value in coefs[-2::-1]:
        total = total * x + value
    return total


def across(left, right):
    return lax.dot_general(
        left, right, (((1,), (1,)), ((), ())), preferred_element_type=jnp.float32
    )


def fused_kernel(
    sizes,
    volt_ref,
    pos_hbm,
    dir_hbm,
    basis_hbm,
    rank_hbm,
    out_ref,
    pos_ref,
    dir_ref,
    basis_ref,
    rank_ref,
    turned,
    packed,
    basis_in,
    rows_real,
    rows_imag,
    ortho_real,
    ortho_imag,
    ortho_half,
    steer_real,
    steer_imag,
    weight_real,
    weight_imag,
    power_out,
    power_in,
    local_sem,
    stage_sem,
    volt_send,
    volt_recv,
    basis_send,
    basis_recv,
    power_send,
    power_recv,
):
    inp_size, chan_size, per_chan, beam_count, frames_dev = sizes
    devices = inp_size * chan_size
    local_inputs = volt_ref.shape[2]
    input_count = pos_ref.shape[1]
    ranks = basis_ref.shape[2]
    my_inp = lax.axis_index("inp")
    my_chan = lax.axis_index("chan")
    me = my_inp * chan_size + my_chan
    sub = my_inp // FGROUPS
    samples = frames_dev // DS
    beams_each = beam_count // inp_size
    owners = FORM_ROWS // beams_each
    blocks = beam_count // ROWS
    form_blocks = beam_count // FORM_ROWS
    place = lax.rem(my_inp, FGROUPS)
    half = devices // per_chan

    def device(number):
        return (number // chan_size, lax.rem(number, chan_size))

    def other(k):
        return lax.rem(me + k, devices)

    def other_inp(k):
        return lax.rem(my_inp + k, inp_size)

    pairs = (
        (basis_hbm, basis_ref),
        (pos_hbm, pos_ref),
        (dir_hbm, dir_ref),
        (rank_hbm, rank_ref),
    )
    staged = [
        pltpu.make_async_copy(far, near, stage_sem.at[index])
        for index, (far, near) in enumerate(pairs)
    ]
    for copy in staged:
        copy.start()

    def spread(k):
        target_sub = lax.rem(sub + 1 + k // half, per_chan)
        return target_sub * half + lax.rem(me + k, half)

    barrier = pltpu.get_barrier_semaphore()

    def greet(k, carry):
        pl.semaphore_signal(barrier, inc=1, device_id=device(other(k)), device_id_type=MESH)
        return carry

    lax.fori_loop(1, devices, greet, 0)
    staged[0].wait()
    for index in range(per_chan):
        packed[index] = jnp.concatenate([basis_ref[0, index], basis_ref[1, index]], axis=1)
    basis_in[my_inp] = packed[sub]
    pl.semaphore_wait(barrier, devices - 1)

    def basis_cross(target_sub, slot):
        target = target_sub * FGROUPS + place
        return pltpu.make_async_remote_copy(
            src_ref=packed.at[target_sub],
            dst_ref=basis_in.at[slot],
            send_sem=basis_send.at[target],
            recv_sem=basis_recv.at[slot],
            device_id=(target, my_chan),
            device_id_type=MESH,
        )

    def basis_near(slot, peer):
        return pltpu.make_async_remote_copy(
            src_ref=basis_in.at[slot],
            dst_ref=basis_in.at[slot],
            send_sem=basis_send.at[slot // FGROUPS * FGROUPS + peer],
            recv_sem=basis_recv.at[slot],
            device_id=(sub * FGROUPS + peer, my_chan),
            device_id_type=MESH,
        )

    def peer(k):
        return lax.rem(place + k, FGROUPS)

    def volt_block(target):
        target_inp = target // chan_size
        channel = lax.rem(target, chan_size) * per_chan + target_inp // FGROUPS
        start = pl.multiple_of(lax.rem(target_inp, FGROUPS) * frames_dev, frames_dev)
        return volt_ref.at[:, channel, :, pl.ds(start, frames_dev)]

    def turned_block(slot):
        return turned.at[
            :, pl.ds(pl.multiple_of(slot * local_inputs, local_inputs), local_inputs), :
        ]

    def volt_copy(target, slot):
        return pltpu.make_async_remote_copy(
            src_ref=volt_block(target),
            dst_ref=turned_block(slot),
            send_sem=volt_send.at[target],
            recv_sem=volt_recv.at[slot],
            device_id=device(target),
            device_id_type=MESH,
        )

    def power_copy(target, slot):
        return pltpu.make_async_remote_copy(
            src_ref=power_out.at[target],
            dst_ref=power_in.at[slot],
            send_sem=power_send.at[target],
            recv_sem=power_recv.at[slot],
            device_id=(target, my_chan),
            device_id_type=MESH,
        )

    for offset in range(1, per_chan):
        basis_cross(lax.rem(sub + offset, per_chan), my_inp).start()

    def pass_basis(slot):
        def body(k, carry):
            basis_near(slot, peer(k)).start()
            return carry

        lax.fori_loop(1, FGROUPS, body, 0)

    pass_basis(my_inp)

    def send_volt(k, carry):
        volt_copy(spread(k), me).start()
        return carry

    lax.fori_loop(0, FIRST_SENDS, send_volt, 0)
    for offset in range(1, per_chan):
        source = lax.rem(sub + offset, per_chan) * FGROUPS + place
        basis_near(source, place).wait_recv()
        pass_basis(source)
    lax.fori_loop(FIRST_SENDS, devices - half, send_volt, 0)
    lax.fori_loop(devices - half + 1, devices, send_volt, 0)
    own = pltpu.make_async_copy(volt_block(me), turned_block(me), local_sem)
    own.start()
    for copy in staged[1:]:
        copy.wait()

    channel = my_chan * per_chan + sub
    frequency = 1.0 + 0.5 * channel.astype(jnp.float32) / (chan_size * per_chan)
    sin_coefs, cos_coefs = turn_coefficients(input_count)

    def steer(block, carry):
        rows = pl.ds(pl.multiple_of(block * ROWS, ROWS), ROWS)
        first = jnp.broadcast_to(dir_ref[0:1, rows], (ROWS, ROWS)).T
        second = jnp.broadcast_to(dir_ref[1:2, rows], (ROWS, ROWS)).T
        for piece in range(input_count // ROWS):
            lanes = slice(piece * ROWS, (piece + 1) * ROWS)
            turns = first * (pos_ref[0:1, lanes] * frequency) + second * (
                pos_ref[1:2, lanes] * frequency
            )
            turns = turns - jnp.round(turns)
            square = turns * turns
            steer_real[rows, lanes] = horner(cos_coefs, square)
            steer_imag[rows, lanes] = -turns * horner(sin_coefs, square)
        return carry

    lax.fori_loop(0, blocks, steer, 0)

    def take_basis(index, carry):
        slot = index // (FGROUPS - 1) * FGROUPS + peer(lax.rem(index, FGROUPS - 1) + 1)
        basis_near(slot, place).wait_recv()
        return carry

    lax.fori_loop(0, per_chan * (FGROUPS - 1), take_basis, 0)
    lanes_each = basis_ref.shape[3]
    rows_real[...] = jnp.concatenate([basis_in[s, :, :lanes_each] for s in range(inp_size)], axis=1)
    rows_imag[...] = jnp.concatenate([basis_in[s, :, lanes_each:] for s in range(inp_size)], axis=1)
    ortho_real[...] = jnp.zeros_like(ortho_real)
    ortho_imag[...] = jnp.zeros_like(ortho_imag)
    rank_used = rank_ref[sub]

    def build_row(row, carry):
        real_part = rows_real[pl.ds(row, 1), :]
        imag_part = rows_imag[pl.ds(row, 1), :]
        for second in range(2):
            real_rows, imag_rows = ortho_real[...], ortho_imag[...]
            coef_real = jnp.sum(
                real_rows * real_part + imag_rows * imag_part, axis=1, keepdims=True
            )
            coef_imag = jnp.sum(
                real_rows * imag_part - imag_rows * real_part, axis=1, keepdims=True
            )
            real_part = real_part - jnp.sum(
                coef_real * real_rows - coef_imag * imag_rows, axis=0, keepdims=True
            )
            imag_part = imag_part - jnp.sum(
                coef_real * imag_rows + coef_imag * real_rows, axis=0, keepdims=True
            )
        flag = jnp.where(row < rank_used, 1.0, 0.0).astype(jnp.float32)
        square = jnp.sum(
            real_part * real_part + imag_part * imag_part, axis=1, keepdims=True
        )
        normalize = flag / jnp.sqrt(square + (1.0 - flag))
        ortho_real[pl.ds(row, 1), :] = real_part * normalize
        ortho_imag[pl.ds(row, 1), :] = imag_part * normalize
        return carry

    lax.fori_loop(0, ranks, build_row, 0)
    ortho_half[...] = jnp.concatenate([ortho_real[...], ortho_imag[...]], axis=0).astype(
        jnp.bfloat16
    )

    def project(block, carry):
        rows = pl.ds(pl.multiple_of(block * FORM_ROWS, FORM_ROWS), FORM_ROWS)
        half_rows = ortho_half[...]
        from_real = across(steer_real[rows, :].astype(jnp.bfloat16), half_rows)
        from_imag = across(steer_imag[rows, :].astype(jnp.bfloat16), half_rows)
        along_real = from_real[:, :ranks] - from_imag[:, ranks:]
        along_imag = from_real[:, ranks:] + from_imag[:, :ranks]
        for_real = jnp.concatenate([along_real, along_imag], axis=1).astype(jnp.bfloat16)
        for_imag = jnp.concatenate([along_imag, -along_real], axis=1).astype(jnp.bfloat16)
        weight_real[rows, :] = (steer_real[rows, :] - half_dot(for_real, half_rows)).astype(
            jnp.bfloat16
        )
        weight_imag[rows, :] = (steer_imag[rows, :] - half_dot(for_imag, half_rows)).astype(
            jnp.bfloat16
        )
        return carry

    lax.fori_loop(0, form_blocks, project, 0)

    depth = half * local_inputs

    def beams(rows, group):
        start = pl.multiple_of(group * depth, depth)
        left = weight_real[rows, pl.ds(start, depth)]
        right = weight_imag[rows, pl.ds(start, depth)]
        volt_real = turned[0, pl.ds(start, depth), :]
        volt_imag = turned[1, pl.ds(start, depth), :]
        return (
            half_dot(left, volt_real) - half_dot(right, volt_imag),
            half_dot(left, volt_imag) + half_dot(right, volt_real),
        )

    def take_group(offset):
        group = lax.rem(sub + offset, per_chan)

        def take_volt(k, carry):
            source = group * half + lax.rem(me + k, half)
            volt_copy(source, source).wait_recv()
            return carry

        if offset == 0:
            own.wait()
        lax.fori_loop(1 if offset == 0 else 0, half, take_volt, 0)
        return group

    for offset in range(per_chan - 1):
        early = take_group(offset)

        def form_early(block, carry):
            rows = pl.ds(pl.multiple_of(block * FORM_ROWS, FORM_ROWS), FORM_ROWS)
            beam_real, beam_imag = beams(rows, early)
            if offset > 0:
                beam_real = beam_real + steer_real[rows, :frames_dev]
                beam_imag = beam_imag + steer_imag[rows, :frames_dev]
            steer_real[rows, :frames_dev] = beam_real
            steer_imag[rows, :frames_dev] = beam_imag
            return carry

        lax.fori_loop(0, form_blocks, form_early, 0)
    last = take_group(per_chan - 1)

    sample_row = lax.broadcasted_iota(jnp.int32, (samples, frames_dev), 0)
    frame_column = lax.broadcasted_iota(jnp.int32, (samples, frames_dev), 1)
    inside = (frame_column >= sample_row * DS) & (frame_column < sample_row * DS + DS)
    pool = jnp.where(inside, 1.0 / DS, 0.0).astype(jnp.bfloat16)

    def form(step, carry):
        block = lax.rem(step + my_inp // owners + 1, form_blocks)
        rows = pl.ds(pl.multiple_of(block * FORM_ROWS, FORM_ROWS), FORM_ROWS)
        beam_real, beam_imag = beams(rows, last)
        if per_chan > 1:
            beam_real = beam_real + steer_real[rows, :frames_dev]
            beam_imag = beam_imag + steer_imag[rows, :frames_dev]
        power = beam_real * beam_real + beam_imag * beam_imag
        high = power.astype(jnp.bfloat16)
        rest = power - high.astype(jnp.float32)
        middle = rest.astype(jnp.bfloat16)
        low = (rest - middle.astype(jnp.float32)).astype(jnp.bfloat16)
        binned = across(pool, high) + across(pool, middle) + across(pool, low)
        for part in range(owners):
            target = block * owners + part
            wide = binned[:, part * beams_each : (part + 1) * beams_each]
            piece = jnp.concatenate([wide[: samples // 2], wide[samples // 2 :]], axis=1)

            @pl.when(target == my_inp)
            def keep():
                power_in[my_inp] = piece

            @pl.when(target != my_inp)
            def pass_on():
                power_out[target] = piece
                power_copy(target, my_inp).start()

        return carry

    lax.fori_loop(0, form_blocks, form, 0)

    def take_power(k, carry):
        power_copy(other_inp(k), other_inp(k)).wait_recv()
        return carry

    lax.fori_loop(1, inp_size, take_power, 0)
    for index in range(per_chan):
        group = []
        for f in range(FGROUPS):
            piece = power_in[index * FGROUPS + f]
            group += [piece[:, :beams_each], piece[:, beams_each:]]
        out_ref[index] = jnp.concatenate(group, axis=0).T

    def finish_inp(k, carry):
        power_copy(other_inp(k), my_inp).wait_send()
        return carry

    lax.fori_loop(1, inp_size, finish_inp, 0)
    for offset in range(1, per_chan):
        basis_cross(lax.rem(sub + offset, per_chan), my_inp).wait_send()

    def finish_basis(index, carry):
        slot = index // (FGROUPS - 1) * FGROUPS + place
        basis_near(slot, peer(lax.rem(index, FGROUPS - 1) + 1)).wait_send()
        return carry

    lax.fori_loop(0, per_chan * (FGROUPS - 1), finish_basis, 0)

    def finish_volt(k, carry):
        volt_copy(other(k), me).wait_send()
        return carry

    lax.fori_loop(1, devices, finish_volt, 0)


def fused(voltages, positions, directions, basis, rank_count):
    inp_size = lax.axis_size("inp")
    chan_size = lax.axis_size("chan")
    devices = inp_size * chan_size
    per_chan = inp_size // FGROUPS
    frames_dev = voltages.shape[3] // FGROUPS
    input_count = positions.shape[0]
    beam_count = directions.shape[0]
    ranks = basis.shape[2]
    basis_lanes = basis.shape[3]
    samples = frames_dev // DS
    beams_each = beam_count // inp_size
    sizes = (inp_size, chan_size, per_chan, beam_count, frames_dev)
    vmem = pl.BlockSpec(memory_space=pltpu.VMEM)
    dma = pltpu.SemaphoreType.DMA
    row_block = pltpu.VMEM((ranks, input_count), jnp.float32)
    weight = pltpu.VMEM((beam_count, input_count), jnp.bfloat16)
    wave = pltpu.VMEM((beam_count, input_count), jnp.float32)
    result = pl.pallas_call(
        functools.partial(fused_kernel, sizes),
        out_shape=jax.ShapeDtypeStruct(
            (per_chan, beams_each, FGROUPS * samples), jnp.float32
        ),
        in_specs=[pl.BlockSpec(memory_space=pl.ANY)] * 5,
        out_specs=vmem,
        scratch_shapes=[
            pltpu.VMEM((2, input_count), jnp.float32),
            pltpu.VMEM((2, beam_count), jnp.float32),
            pltpu.VMEM(basis.shape, jnp.float32),
            pltpu.SMEM(rank_count.shape, jnp.int32),
            pltpu.VMEM((2, input_count, frames_dev), jnp.bfloat16),
            pltpu.VMEM((per_chan, ranks, 2 * basis_lanes), jnp.float32),
            pltpu.VMEM((inp_size, ranks, 2 * basis_lanes), jnp.float32),
            row_block,
            row_block,
            row_block,
            row_block,
            pltpu.VMEM((2 * ranks, input_count), jnp.bfloat16),
            wave,
            wave,
            weight,
            weight,
            pltpu.VMEM((inp_size, samples // 2, 2 * beams_each), jnp.float32),
            pltpu.VMEM((inp_size, samples // 2, 2 * beams_each), jnp.float32),
            dma,
            dma((4,)),
            dma((devices,)),
            dma((devices,)),
            dma((inp_size,)),
            dma((inp_size,)),
            dma((inp_size,)),
            dma((inp_size,)),
        ],
        compiler_params=pltpu.CompilerParams(
            collective_id=0, has_side_effects=True, vmem_limit_bytes=60 * 1024 * 1024
        ),
    )(voltages, positions.T, directions.T, basis, rank_count)
    return jnp.transpose(result, (1, 0, 2))


def fits(mesh_sizes, voltages, positions, directions):
    inp_size, chan_size = mesh_sizes
    beams_each = directions.shape[0] // inp_size
    return (
        voltages.shape[2] % 16 == 0
        and (voltages.shape[3] // FGROUPS) % 128 == 0
        and positions.shape[0] % ROWS == 0
        and directions.shape[0] % FORM_ROWS == 0
        and positions.shape[0] >= voltages.shape[3] // FGROUPS
        and (inp_size * chan_size * voltages.shape[2]) == positions.shape[0]
        and inp_size % FGROUPS == 0
        and FGROUPS * chan_size * voltages.shape[2] % 128 == 0
        and FORM_ROWS % beams_each == 0
    )


def either(voltages, positions, directions, basis, rank_count):
    mesh_sizes = (lax.axis_size("inp"), lax.axis_size("chan"))
    way = fused if fits(mesh_sizes, voltages, positions, directions) else shards
    return way(voltages, positions, directions, basis, rank_count)


def solution(mesh):
    placed = (
        P(None, None, ("inp", "chan"), None),
        P(),
        P(),
        P(None, "chan", None, "inp"),
        P("chan"),
    )
    return jax.shard_map(
        either, mesh=mesh, in_specs=placed, out_specs=P("inp", "chan", None), check_vma=False
    )
```

```python
import functools
import math

import jax
import jax.numpy as jnp
import numpy as np
from jax import lax
from jax.experimental import pallas as pl
from jax.experimental.pallas import tpu as pltpu
from jax.sharding import PartitionSpec as P

FGROUPS = 8
DS = 16
ROWS = 128
FORM_ROWS = 512
FIRST_SENDS = 2
MESH = pl.DeviceIdType.MESH


HIGHEST_PRECISION = lax.Precision.HIGHEST


def orthonormal(basis_rows, rank_used):
    ranks = basis_rows.shape[1]
    active = (jnp.arange(ranks) < rank_used).astype(basis_rows.dtype)

    def build_column(column_index, ortho_rows):
        real_part = lax.dynamic_index_in_dim(basis_rows[0], column_index, 0, keepdims=False)
        imag_part = lax.dynamic_index_in_dim(basis_rows[1], column_index, 0, keepdims=False)
        for second in range(2):
            coef_real = jnp.dot(ortho_rows[0], real_part, precision=HIGHEST_PRECISION) + jnp.dot(
                ortho_rows[1], imag_part, precision=HIGHEST_PRECISION
            )
            coef_imag = jnp.dot(ortho_rows[0], imag_part, precision=HIGHEST_PRECISION) - jnp.dot(
                ortho_rows[1], real_part, precision=HIGHEST_PRECISION
            )
            real_part = real_part - (
                jnp.dot(coef_real, ortho_rows[0], precision=HIGHEST_PRECISION)
                - jnp.dot(coef_imag, ortho_rows[1], precision=HIGHEST_PRECISION)
            )
            imag_part = imag_part - (
                jnp.dot(coef_real, ortho_rows[1], precision=HIGHEST_PRECISION)
                + jnp.dot(coef_imag, ortho_rows[0], precision=HIGHEST_PRECISION)
            )
        flag = lax.dynamic_index_in_dim(active, column_index, 0, keepdims=False)
        normalize = flag / jnp.sqrt(
            jnp.sum(real_part * real_part + imag_part * imag_part) + (1.0 - flag)
        )
        new_column = jnp.stack([real_part * normalize, imag_part * normalize])[:, None, :]
        return lax.dynamic_update_slice_in_dim(ortho_rows, new_column, column_index, 1)

    return lax.fori_loop(0, ranks, build_column, jnp.zeros_like(basis_rows))


def half_dot(left, right):
    return jnp.dot(left, right, preferred_element_type=jnp.float32)


def steer_block(row_start, row_count, positions, directions, ortho_rows, frequency):
    chosen = lax.dynamic_slice_in_dim(directions, row_start, row_count, 0)
    phase_angle = (
        2.0
        * jnp.pi
        * frequency
        * (chosen[:, 0:1] * positions[:, 0][None, :] + chosen[:, 1:2] * positions[:, 1][None, :])
    )
    inverse = 1.0 / math.sqrt(positions.shape[0])
    steer_real = jnp.cos(phase_angle) * inverse
    steer_imag = -jnp.sin(phase_angle) * inverse
    short_real = steer_real.astype(jnp.bfloat16)
    short_imag = steer_imag.astype(jnp.bfloat16)
    ortho_real = ortho_rows[0].astype(jnp.bfloat16)
    ortho_imag = ortho_rows[1].astype(jnp.bfloat16)
    along_real = (half_dot(short_real, ortho_real.T) - half_dot(short_imag, ortho_imag.T)).astype(
        jnp.bfloat16
    )
    along_imag = (half_dot(short_real, ortho_imag.T) + half_dot(short_imag, ortho_real.T)).astype(
        jnp.bfloat16
    )
    kept_real = steer_real - (half_dot(along_real, ortho_real) + half_dot(along_imag, ortho_imag))
    kept_imag = steer_imag - (half_dot(along_imag, ortho_real) - half_dot(along_real, ortho_imag))
    return (kept_real.astype(jnp.bfloat16), kept_imag.astype(jnp.bfloat16))


def projected_weights(positions, directions, ortho_rows, frequency):
    beam_count = directions.shape[0]
    row_count = min(beam_count, 512)
    block_count = beam_count // row_count

    def one_block(block_index):
        return steer_block(
            block_index * row_count, row_count, positions, directions, ortho_rows, frequency
        )

    weight_real, weight_imag = lax.map(one_block, jnp.arange(block_count, dtype=jnp.int32))
    input_count = positions.shape[0]
    return (
        weight_real.reshape(beam_count, input_count),
        weight_imag.reshape(beam_count, input_count),
    )


def detect(weight_real, weight_imag, volt_real, volt_imag):
    stacked = jnp.concatenate([volt_real, volt_imag], axis=1)
    frame_count = volt_real.shape[1]
    from_real = jnp.dot(weight_real, stacked, preferred_element_type=jnp.float32)
    from_imag = jnp.dot(weight_imag, stacked, preferred_element_type=jnp.float32)
    beam_real = from_real[:, :frame_count] - from_imag[:, frame_count:]
    beam_imag = from_real[:, frame_count:] + from_imag[:, :frame_count]
    return beam_real * beam_real + beam_imag * beam_imag


def shards(voltages, positions, directions, basis, rank_count):
    inp_size = lax.axis_size("inp")
    chan_size = lax.axis_size("chan")
    per_chan = inp_size // FGROUPS
    channels = chan_size * per_chan
    local_inputs = voltages.shape[2]
    frames_dev = voltages.shape[3] // FGROUPS
    input_count = positions.shape[0]
    beam_count = directions.shape[0]
    sub_channel = lax.axis_index("inp") // FGROUPS
    channel = lax.axis_index("chan") * per_chan + sub_channel
    frequency = 1.0 + 0.5 * channel.astype(jnp.float32) / channels
    rank_used = jnp.sum(jnp.where(jnp.arange(per_chan) == sub_channel, rank_count, 0))
    group_basis = lax.all_gather(basis, "inp", axis=3, tiled=True)
    own_basis = lax.dynamic_index_in_dim(group_basis, sub_channel, 1, keepdims=False)
    sectioned = voltages.reshape(2, chan_size, per_chan, local_inputs, FGROUPS, frames_dev)
    sectioned = jnp.transpose(sectioned, (0, 1, 2, 4, 3, 5)).reshape(
        2, chan_size, inp_size, local_inputs, frames_dev
    )
    ordered_positions = jnp.transpose(
        positions.reshape(inp_size, chan_size, local_inputs, 2), (1, 0, 2, 3)
    ).reshape(input_count, 2)
    ordered_basis = own_basis.reshape(2, own_basis.shape[1], inp_size, chan_size, local_inputs)
    ordered_basis = jnp.transpose(ordered_basis, (0, 1, 3, 2, 4)).reshape(
        2, own_basis.shape[1], input_count
    )
    ortho_rows = orthonormal(ordered_basis, rank_used)
    weight_real, weight_imag = projected_weights(
        ordered_positions, directions, ortho_rows, frequency
    )
    turned = lax.all_to_all(
        lax.all_to_all(sectioned, "inp", split_axis=2, concat_axis=3, tiled=True),
        "chan",
        split_axis=1,
        concat_axis=3,
        tiled=True,
    )
    detected = detect(weight_real, weight_imag, turned[0, 0, 0], turned[1, 0, 0])
    binned = jnp.mean(detected.reshape(beam_count, frames_dev // DS, DS), axis=2)
    regrouped = lax.all_to_all(binned[:, None, :], "inp", split_axis=0, concat_axis=1, tiled=True)
    return regrouped.reshape(beam_count // inp_size, per_chan, FGROUPS * (frames_dev // DS))


def turn_coefficients(input_count):
    nodes = np.cos(np.pi * (np.arange(400) + 0.5) / 400) * 0.25 * 0.5 + 0.125
    root = np.sqrt(nodes)
    scale = 1.0 / math.sqrt(input_count)
    fit = np.polynomial.chebyshev.Chebyshev.fit
    power = np.polynomial.Polynomial
    sin_fit = fit(nodes, np.sin(2 * np.pi * root) / root, 5, domain=[0, 0.25]).convert(kind=power)
    cos_fit = fit(nodes, np.cos(2 * np.pi * root), 6, domain=[0, 0.25]).convert(kind=power)
    return (
        [float(value) * scale for value in sin_fit.coef],
        [float(value) * scale for value in cos_fit.coef],
    )


def horner(coefs, x):
    total = jnp.full_like(x, coefs[-1])
    for value in coefs[-2::-1]:
        total = total * x + value
    return total


def across(left, right):
    return lax.dot_general(
        left, right, (((1,), (1,)), ((), ())), preferred_element_type=jnp.float32
    )


def fused_kernel(
    sizes,
    volt_ref,
    pos_hbm,
    dir_hbm,
    basis_hbm,
    rank_hbm,
    out_ref,
    pos_ref,
    dir_ref,
    basis_ref,
    rank_ref,
    turned,
    packed,
    basis_in,
    rows_real,
    rows_imag,
    ortho_real,
    ortho_imag,
    ortho_half,
    steer_real,
    steer_imag,
    weight_real,
    weight_imag,
    power_out,
    power_in,
    local_sem,
    stage_sem,
    volt_send,
    volt_recv,
    basis_send,
    basis_recv,
    power_send,
    power_recv,
):
    inp_size, chan_size, per_chan, beam_count, frames_dev = sizes
    devices = inp_size * chan_size
    local_inputs = volt_ref.shape[2]
    input_count = pos_ref.shape[1]
    ranks = basis_ref.shape[2]
    my_inp = lax.axis_index("inp")
    my_chan = lax.axis_index("chan")
    me = my_inp * chan_size + my_chan
    sub = my_inp // FGROUPS
    samples = frames_dev // DS
    beams_each = beam_count // inp_size
    owners = FORM_ROWS // beams_each
    blocks = beam_count // ROWS
    form_blocks = beam_count // FORM_ROWS
    place = lax.rem(my_inp, FGROUPS)
    half = devices // per_chan

    def device(number):
        return (number // chan_size, lax.rem(number, chan_size))

    def other(k):
        return lax.rem(me + k, devices)

    def other_inp(k):
        return lax.rem(my_inp + k, inp_size)

    pairs = (
        (basis_hbm, basis_ref),
        (pos_hbm, pos_ref),
        (dir_hbm, dir_ref),
        (rank_hbm, rank_ref),
    )
    staged = [
        pltpu.make_async_copy(far, near, stage_sem.at[index])
        for index, (far, near) in enumerate(pairs)
    ]
    for copy in staged:
        copy.start()

    def spread(k):
        target_sub = lax.rem(sub + 1 + k // half, per_chan)
        return target_sub * half + lax.rem(me + k, half)

    barrier = pltpu.get_barrier_semaphore()

    def greet(k, carry):
        pl.semaphore_signal(barrier, inc=1, device_id=device(other(k)), device_id_type=MESH)
        return carry

    lax.fori_loop(1, devices, greet, 0)
    staged[0].wait()
    for index in range(per_chan):
        packed[index] = jnp.concatenate([basis_ref[0, index], basis_ref[1, index]], axis=1)
    basis_in[my_inp] = packed[sub]
    pl.semaphore_wait(barrier, devices - 1)

    def basis_cross(target_sub, slot):
        target = target_sub * FGROUPS + place
        return pltpu.make_async_remote_copy(
            src_ref=packed.at[target_sub],
            dst_ref=basis_in.at[slot],
            send_sem=basis_send.at[target],
            recv_sem=basis_recv.at[slot],
            device_id=(target, my_chan),
            device_id_type=MESH,
        )

    def basis_near(slot, peer):
        return pltpu.make_async_remote_copy(
            src_ref=basis_in.at[slot],
            dst_ref=basis_in.at[slot],
            send_sem=basis_send.at[slot // FGROUPS * FGROUPS + peer],
            recv_sem=basis_recv.at[slot],
            device_id=(sub * FGROUPS + peer, my_chan),
            device_id_type=MESH,
        )

    def peer(k):
        return lax.rem(place + k, FGROUPS)

    def volt_block(target):
        target_inp = target // chan_size
        channel = lax.rem(target, chan_size) * per_chan + target_inp // FGROUPS
        start = pl.multiple_of(lax.rem(target_inp, FGROUPS) * frames_dev, frames_dev)
        return volt_ref.at[:, channel, :, pl.ds(start, frames_dev)]

    def turned_block(slot):
        return turned.at[
            :, pl.ds(pl.multiple_of(slot * local_inputs, local_inputs), local_inputs), :
        ]

    def volt_copy(target, slot):
        return pltpu.make_async_remote_copy(
            src_ref=volt_block(target),
            dst_ref=turned_block(slot),
            send_sem=volt_send.at[target],
            recv_sem=volt_recv.at[slot],
            device_id=device(target),
            device_id_type=MESH,
        )

    def power_copy(target, slot):
        return pltpu.make_async_remote_copy(
            src_ref=power_out.at[target],
            dst_ref=power_in.at[slot],
            send_sem=power_send.at[target],
            recv_sem=power_recv.at[slot],
            device_id=(target, my_chan),
            device_id_type=MESH,
        )

    for offset in range(1, per_chan):
        basis_cross(lax.rem(sub + offset, per_chan), my_inp).start()

    def pass_basis(slot):
        def body(k, carry):
            basis_near(slot, peer(k)).start()
            return carry

        lax.fori_loop(1, FGROUPS, body, 0)

    pass_basis(my_inp)

    def send_volt(k, carry):
        volt_copy(spread(k), me).start()
        return carry

    lax.fori_loop(0, FIRST_SENDS, send_volt, 0)
    for offset in range(1, per_chan):
        source = lax.rem(sub + offset, per_chan) * FGROUPS + place
        basis_near(source, place).wait_recv()
        pass_basis(source)
    lax.fori_loop(FIRST_SENDS, devices - half, send_volt, 0)
    lax.fori_loop(devices - half + 1, devices, send_volt, 0)
    own = pltpu.make_async_copy(volt_block(me), turned_block(me), local_sem)
    own.start()
    for copy in staged[1:]:
        copy.wait()

    channel = my_chan * per_chan + sub
    frequency = 1.0 + 0.5 * channel.astype(jnp.float32) / (chan_size * per_chan)
    sin_coefs, cos_coefs = turn_coefficients(input_count)

    def steer(block, carry):
        rows = pl.ds(pl.multiple_of(block * ROWS, ROWS), ROWS)
        first = jnp.broadcast_to(dir_ref[0:1, rows], (ROWS, ROWS)).T
        second = jnp.broadcast_to(dir_ref[1:2, rows], (ROWS, ROWS)).T
        for piece in range(input_count // ROWS):
            lanes = slice(piece * ROWS, (piece + 1) * ROWS)
            turns = first * (pos_ref[0:1, lanes] * frequency) + second * (
                pos_ref[1:2, lanes] * frequency
            )
            turns = turns - jnp.round(turns)
            square = turns * turns
            steer_real[rows, lanes] = horner(cos_coefs, square)
            steer_imag[rows, lanes] = -turns * horner(sin_coefs, square)
        return carry

    lax.fori_loop(0, blocks, steer, 0)

    def take_basis(index, carry):
        slot = index // (FGROUPS - 1) * FGROUPS + peer(lax.rem(index, FGROUPS - 1) + 1)
        basis_near(slot, place).wait_recv()
        return carry

    lax.fori_loop(0, per_chan * (FGROUPS - 1), take_basis, 0)
    lanes_each = basis_ref.shape[3]
    rows_real[...] = jnp.concatenate([basis_in[s, :, :lanes_each] for s in range(inp_size)], axis=1)
    rows_imag[...] = jnp.concatenate([basis_in[s, :, lanes_each:] for s in range(inp_size)], axis=1)
    ortho_real[...] = jnp.zeros_like(ortho_real)
    ortho_imag[...] = jnp.zeros_like(ortho_imag)
    rank_used = rank_ref[sub]

    def build_row(row, carry):
        real_part = rows_real[pl.ds(row, 1), :]
        imag_part = rows_imag[pl.ds(row, 1), :]
        for second in range(2):
            real_rows, imag_rows = ortho_real[...], ortho_imag[...]
            coef_real = jnp.sum(
                real_rows * real_part + imag_rows * imag_part, axis=1, keepdims=True
            )
            coef_imag = jnp.sum(
                real_rows * imag_part - imag_rows * real_part, axis=1, keepdims=True
            )
            real_part = real_part - jnp.sum(
                coef_real * real_rows - coef_imag * imag_rows, axis=0, keepdims=True
            )
            imag_part = imag_part - jnp.sum(
                coef_real * imag_rows + coef_imag * real_rows, axis=0, keepdims=True
            )
        flag = jnp.where(row < rank_used, 1.0, 0.0).astype(jnp.float32)
        square = jnp.sum(
            real_part * real_part + imag_part * imag_part, axis=1, keepdims=True
        )
        normalize = flag / jnp.sqrt(square + (1.0 - flag))
        ortho_real[pl.ds(row, 1), :] = real_part * normalize
        ortho_imag[pl.ds(row, 1), :] = imag_part * normalize
        return carry

    lax.fori_loop(0, ranks, build_row, 0)
    ortho_half[...] = jnp.concatenate([ortho_real[...], ortho_imag[...]], axis=0).astype(
        jnp.bfloat16
    )

    def project(block, carry):
        rows = pl.ds(pl.multiple_of(block * FORM_ROWS, FORM_ROWS), FORM_ROWS)
        half_rows = ortho_half[...]
        from_real = across(steer_real[rows, :].astype(jnp.bfloat16), half_rows)
        from_imag = across(steer_imag[rows, :].astype(jnp.bfloat16), half_rows)
        along_real = from_real[:, :ranks] - from_imag[:, ranks:]
        along_imag = from_real[:, ranks:] + from_imag[:, :ranks]
        for_real = jnp.concatenate([along_real, along_imag], axis=1).astype(jnp.bfloat16)
        for_imag = jnp.concatenate([along_imag, -along_real], axis=1).astype(jnp.bfloat16)
        weight_real[rows, :] = (steer_real[rows, :] - half_dot(for_real, half_rows)).astype(
            jnp.bfloat16
        )
        weight_imag[rows, :] = (steer_imag[rows, :] - half_dot(for_imag, half_rows)).astype(
            jnp.bfloat16
        )
        return carry

    lax.fori_loop(0, form_blocks, project, 0)

    depth = half * local_inputs

    def beams(rows, group):
        start = pl.multiple_of(group * depth, depth)
        left = weight_real[rows, pl.ds(start, depth)]
        right = weight_imag[rows, pl.ds(start, depth)]
        volt_real = turned[0, pl.ds(start, depth), :]
        volt_imag = turned[1, pl.ds(start, depth), :]
        return (
            half_dot(left, volt_real) - half_dot(right, volt_imag),
            half_dot(left, volt_imag) + half_dot(right, volt_real),
        )

    def take_group(offset):
        group = lax.rem(sub + offset, per_chan)

        def take_volt(k, carry):
            source = group * half + lax.rem(me + k, half)
            volt_copy(source, source).wait_recv()
            return carry

        if offset == 0:
            own.wait()
        lax.fori_loop(1 if offset == 0 else 0, half, take_volt, 0)
        return group

    for offset in range(per_chan - 1):
        early = take_group(offset)

        def form_early(block, carry):
            rows = pl.ds(pl.multiple_of(block * FORM_ROWS, FORM_ROWS), FORM_ROWS)
            beam_real, beam_imag = beams(rows, early)
            if offset > 0:
                beam_real = beam_real + steer_real[rows, :frames_dev]
                beam_imag = beam_imag + steer_imag[rows, :frames_dev]
            steer_real[rows, :frames_dev] = beam_real
            steer_imag[rows, :frames_dev] = beam_imag
            return carry

        lax.fori_loop(0, form_blocks, form_early, 0)
    last = take_group(per_chan - 1)

    sample_row = lax.broadcasted_iota(jnp.int32, (samples, frames_dev), 0)
    frame_column = lax.broadcasted_iota(jnp.int32, (samples, frames_dev), 1)
    inside = (frame_column >= sample_row * DS) & (frame_column < sample_row * DS + DS)
    pool = jnp.where(inside, 1.0 / DS, 0.0).astype(jnp.bfloat16)

    def form(step, carry):
        block = lax.rem(step + my_inp // owners + 1, form_blocks)
        rows = pl.ds(pl.multiple_of(block * FORM_ROWS, FORM_ROWS), FORM_ROWS)
        beam_real, beam_imag = beams(rows, last)
        if per_chan > 1:
            beam_real = beam_real + steer_real[rows, :frames_dev]
            beam_imag = beam_imag + steer_imag[rows, :frames_dev]
        power = beam_real * beam_real + beam_imag * beam_imag
        high = power.astype(jnp.bfloat16)
        rest = power - high.astype(jnp.float32)
        middle = rest.astype(jnp.bfloat16)
        low = (rest - middle.astype(jnp.float32)).astype(jnp.bfloat16)
        binned = across(pool, high) + across(pool, middle) + across(pool, low)
        for part in range(owners):
            target = block * owners + part
            wide = binned[:, part * beams_each : (part + 1) * beams_each]
            piece = jnp.concatenate([wide[: samples // 2], wide[samples // 2 :]], axis=1)

            @pl.when(target == my_inp)
            def keep():
                power_in[my_inp] = piece

            @pl.when(target != my_inp)
            def pass_on():
                power_out[target] = piece
                power_copy(target, my_inp).start()

        return carry

    lax.fori_loop(0, form_blocks, form, 0)

    def take_power(k, carry):
        power_copy(other_inp(k), other_inp(k)).wait_recv()
        return carry

    lax.fori_loop(1, inp_size, take_power, 0)
    for index in range(per_chan):
        group = []
        for f in range(FGROUPS):
            piece = power_in[index * FGROUPS + f]
            group += [piece[:, :beams_each], piece[:, beams_each:]]
        out_ref[index] = jnp.concatenate(group, axis=0).T

    def finish_inp(k, carry):
        power_copy(other_inp(k), my_inp).wait_send()
        return carry

    lax.fori_loop(1, inp_size, finish_inp, 0)
    for offset in range(1, per_chan):
        basis_cross(lax.rem(sub + offset, per_chan), my_inp).wait_send()

    def finish_basis(index, carry):
        slot = index // (FGROUPS - 1) * FGROUPS + place
        basis_near(slot, peer(lax.rem(index, FGROUPS - 1) + 1)).wait_send()
        return carry

    lax.fori_loop(0, per_chan * (FGROUPS - 1), finish_basis, 0)

    def finish_volt(k, carry):
        volt_copy(other(k), me).wait_send()
        return carry

    lax.fori_loop(1, devices, finish_volt, 0)


def fused(voltages, positions, directions, basis, rank_count):
    inp_size = lax.axis_size("inp")
    chan_size = lax.axis_size("chan")
    devices = inp_size * chan_size
    per_chan = inp_size // FGROUPS
    frames_dev = voltages.shape[3] // FGROUPS
    input_count = positions.shape[0]
    beam_count = directions.shape[0]
    ranks = basis.shape[2]
    basis_lanes = basis.shape[3]
    samples = frames_dev // DS
    beams_each = beam_count // inp_size
    sizes = (inp_size, chan_size, per_chan, beam_count, frames_dev)
    vmem = pl.BlockSpec(memory_space=pltpu.VMEM)
    dma = pltpu.SemaphoreType.DMA
    row_block = pltpu.VMEM((ranks, input_count), jnp.float32)
    weight = pltpu.VMEM((beam_count, input_count), jnp.bfloat16)
    wave = pltpu.VMEM((beam_count, input_count), jnp.float32)
    result = pl.pallas_call(
        functools.partial(fused_kernel, sizes),
        out_shape=jax.ShapeDtypeStruct(
            (per_chan, beams_each, FGROUPS * samples), jnp.float32
        ),
        in_specs=[pl.BlockSpec(memory_space=pl.ANY)] * 5,
        out_specs=vmem,
        scratch_shapes=[
            pltpu.VMEM((2, input_count), jnp.float32),
            pltpu.VMEM((2, beam_count), jnp.float32),
            pltpu.VMEM(basis.shape, jnp.float32),
            pltpu.SMEM(rank_count.shape, jnp.int32),
            pltpu.VMEM((2, input_count, frames_dev), jnp.bfloat16),
            pltpu.VMEM((per_chan, ranks, 2 * basis_lanes), jnp.float32),
            pltpu.VMEM((inp_size, ranks, 2 * basis_lanes), jnp.float32),
            row_block,
            row_block,
            row_block,
            row_block,
            pltpu.VMEM((2 * ranks, input_count), jnp.bfloat16),
            wave,
            wave,
            weight,
            weight,
            pltpu.VMEM((inp_size, samples // 2, 2 * beams_each), jnp.float32),
            pltpu.VMEM((inp_size, samples // 2, 2 * beams_each), jnp.float32),
            dma,
            dma((4,)),
            dma((devices,)),
            dma((devices,)),
            dma((inp_size,)),
            dma((inp_size,)),
            dma((inp_size,)),
            dma((inp_size,)),
        ],
        compiler_params=pltpu.CompilerParams(
            collective_id=0, has_side_effects=True, vmem_limit_bytes=60 * 1024 * 1024
        ),
    )(voltages, positions.T, directions.T, basis, rank_count)
    return jnp.transpose(result, (1, 0, 2))


def fits(mesh_sizes, voltages, positions, directions):
    inp_size, chan_size = mesh_sizes
    beams_each = directions.shape[0] // inp_size
    return (
        voltages.shape[2] % 16 == 0
        and (voltages.shape[3] // FGROUPS) % 128 == 0
        and positions.shape[0] % ROWS == 0
        and directions.shape[0] % FORM_ROWS == 0
        and positions.shape[0] >= voltages.shape[3] // FGROUPS
        and (inp_size * chan_size * voltages.shape[2]) == positions.shape[0]
        and inp_size % FGROUPS == 0
        and FGROUPS * chan_size * voltages.shape[2] % 128 == 0
        and FORM_ROWS % beams_each == 0
    )


def either(voltages, positions, directions, basis, rank_count):
    mesh_sizes = (lax.axis_size("inp"), lax.axis_size("chan"))
    way = fused if fits(mesh_sizes, voltages, positions, directions) else shards
    return way(voltages, positions, directions, basis, rank_count)


def solution(mesh):
    placed = (
        P(None, None, ("inp", "chan"), None),
        P(),
        P(),
        P(None, "chan", None, "inp"),
        P("chan"),
    )
    return jax.shard_map(
        either, mesh=mesh, in_specs=placed, out_specs=P("inp", "chan", None), check_vma=False
    )
```
